1024 devices in a mesh: gx: 8 (over y, core), gy: 32 (over z), gz: 4 (over x).
Axes of the slice: x: 4, y: 4, z: 32, core: 2. Of those that a mesh axis runs over, the one named last changes fastest.
Arguments:
- u_wind: float32 [64, 256, 3072], P('gz', 'gx', 'gy'), may hold values from -6 to 6
- theta: float32 [64, 256, 3072], P('gz', 'gx', 'gy'), may hold values from -6 to 6
- act_points: float32 [4, 8, 32, 1024], P(None, 'gx', 'gy'), may hold values from -8 to 3072, as said below
- point_count: int32 [8, 32], P('gx', 'gy'), may hold values from 1 to 1024, as said below
- klass: int32 [256, 3072], P('gx', 'gy'), may hold values from 0 to 15
- diff_table: float32 [16, 64], replicated, may hold values from 30 to 3000
Outputs:
- u_next: float32 [64, 256, 3072], P('gz', 'gx', 'gy')
- theta_next: float32 [64, 256, 3072], P('gz', 'gx', 'gy')
The draws below stay inside these ranges and needn't reach their ends.
Inputs may be any that keep to these rules, and one draw needn't show every extreme that they name: `act_points`: coordinates of the points of tile (p, q) lie in [p * 32, (p+1) * 32), [q * 96, (q+1) * 96) and [0, 64); the force component lies in [-8, 8]. Only the first point_count[p, q] slots of tile (p, q) are live; the force entries of the other slots are arbitrary values that the weight step masks out. In every draw some tile has all 1024 slots live.
All inputs are finite; a program needn't handle non-finite values.
Results may differ from the reference program's by a relative error of at most 0.0003.
Values sent between devices are 32-bit elements; how exact they have to be, the bound alone decides.
No kernel may reach another device: no remote copies, remote signals or barrier semaphores. Data moves between devices by JAX's collectives and lax.ppermute only.
A program may use at most 32 MiB of HBM per device.

```python
import math
import jax
import jax.numpy as jnp
from jax import lax

CX = 32
CY = 96
HALO = 16
PMAX = 1024
NCLASS = 16
TILES_X = 8
TILES_Y = 32
NX = 256
NY = 3072
NZ = 64


def draw_act_points(key, part):
    key = jax.random.fold_in(key, 11)
    keys = jax.random.split(key, 4)
    shape = (TILES_X, TILES_Y, PMAX)
    tile_x = lax.broadcasted_iota(jnp.int32, shape, 0).astype(jnp.float32)
    tile_y = lax.broadcasted_iota(jnp.int32, shape, 1).astype(jnp.float32)
    pos_x = (tile_x + jax.random.uniform(keys[0], shape, jnp.float32)) * CX
    pos_y = (tile_y + jax.random.uniform(keys[1], shape, jnp.float32)) * CY
    pos_z = jax.random.uniform(keys[2], shape, jnp.float32) * NZ
    push = jnp.clip(3.0 * jax.random.normal(keys[3], shape, jnp.float32), -8.0, 8.0)
    return jnp.stack([pos_x, pos_y, pos_z, push], 0)


def draw_point_count(key, part):
    key = jax.random.fold_in(key, 23)
    keys = jax.random.split(key, 3)
    shape = (TILES_X, TILES_Y)
    first = jax.random.randint(keys[0], shape, 1, PMAX + 1)
    second = jax.random.randint(keys[1], shape, 1, PMAX + 1)
    counts = jnp.maximum(first * second // PMAX, 1)
    pick = jax.random.randint(keys[2], (), 0, TILES_X * TILES_Y)
    flat = jnp.arange(TILES_X * TILES_Y).reshape(shape)
    return jnp.where(flat == pick, PMAX, counts).astype(jnp.int32)


def place_ends(values, rng, smallest, top_value):
    spot = [jax.random.randint(jax.random.fold_in(rng, axis), (), 0, length) for axis, length in enumerate(values.shape)]
    main_axis = values.shape.index(max(values.shape))
    beside = spot[:main_axis] + [(spot[main_axis] + 1) % values.shape[main_axis]] + spot[main_axis + 1:]
    return values.at[tuple(spot)].set(smallest).at[tuple(beside)].set(top_value)


def shard_levels(own_key, extent, shards, low, top_value):
    def one(dim, shards_of):
        draws = jax.random.uniform(jax.random.fold_in(jax.random.fold_in(own_key, 6), dim), (shards_of,), jnp.float32, low / len(shards), top_value / len(shards))
        return jnp.repeat(jnp.exp(draws), extent[dim] // shards_of).reshape((-1,) + (1,) * (len(extent) - dim - 1))

    level = one(*shards[0])
    for cut in shards[1:]:
        level = level * one(*cut)
    return level


def centred(rng, shape, deviation, bound, cuts=(), held_as=jnp.bfloat16):
    result = jax.random.normal(rng, shape, jnp.float32) * deviation
    if len(cuts) > 0:
        result = shard_levels(rng, shape, cuts, -0.22, 0.18) * result
    return jnp.clip(result, min=-bound, max=bound).astype(held_as)


def setup_inputs(seed: int = 0) -> dict:
    arg_keys = jax.random.split(jax.random.key(seed), 7)
    u_wind = centred(arg_keys[0], (NZ, NX, NY), 1.0, 6.0, ((0, 4), (1, 8), (2, 32)), jnp.float32)
    theta = centred(arg_keys[1], (NZ, NX, NY), 1.0, 6.0, ((0, 4), (1, 8), (2, 32)), jnp.float32)
    act_points = draw_act_points(jax.random.fold_in(arg_keys[6], 71), 0)
    point_count = draw_point_count(jax.random.fold_in(arg_keys[6], 71), 0)
    klass = place_ends(jax.random.randint(arg_keys[4], (NX, NY), 0, NCLASS), jax.random.fold_in(arg_keys[4], 1), 0, NCLASS - 1).astype(jnp.int32)
    diff_table = jnp.clip(jnp.exp(jax.random.uniform(arg_keys[5], (NCLASS, NZ), jnp.float32, math.log(30.0), math.log(3000.0))), 30.0, 3000.0)
    return {"u_wind": u_wind, "theta": theta, "act_points": act_points, "point_count": point_count, "klass": klass, "diff_table": diff_table}


HIGH = lax.Precision.HIGHEST
THETA_SCALE = 1.25


def kernel_table(coords, centres, smear):
    offset = (coords[:, None] - centres[None, :]) / smear
    return jnp.exp(-offset * offset)


def tile_force(points, count, tile_x, tile_y):
    smear = HALO / 2.0
    weight = points[3] * (jnp.arange(PMAX) < count).astype(jnp.float32)
    along_x = (tile_x * CX - HALO + jnp.arange(CX + 2 * HALO)).astype(jnp.float32)
    along_y = (tile_y * CY - HALO + jnp.arange(CY + 2 * HALO)).astype(jnp.float32)
    levels = jnp.arange(NZ).astype(jnp.float32)
    kern_x = kernel_table(along_x, points[0], smear)
    kern_y = kernel_table(along_y, points[1], smear).T * weight[:, None]
    kern_z = kernel_table(levels, points[2], smear)
    left = (kern_z[:, None, :] * kern_x[None, :, :]).reshape(NZ * (CX + 2 * HALO), PMAX)
    return jnp.dot(left, kern_y, precision=HIGH).reshape(NZ, CX + 2 * HALO, CY + 2 * HALO)


def project(act_points, point_count):
    padded = jnp.zeros((NZ, NX + 2 * HALO, NY + 2 * HALO), jnp.float32)

    def add_tile(index, padded):
        index = jnp.asarray(index).astype(jnp.int32)
        tile_x = (index // TILES_Y).astype(jnp.int32)
        tile_y = (index % TILES_Y).astype(jnp.int32)
        zero = jnp.zeros((), jnp.int32)
        points = lax.dynamic_slice(act_points, (zero, tile_x, tile_y, zero), (4, 1, 1, PMAX)).reshape(4, PMAX)
        count = lax.dynamic_slice(point_count, (tile_x, tile_y), (1, 1))[0, 0]
        block = tile_force(points, count, tile_x, tile_y)
        starts = (zero, (tile_x * CX).astype(jnp.int32), (tile_y * CY).astype(jnp.int32))
        current = lax.dynamic_slice(padded, starts, block.shape)
        return lax.dynamic_update_slice(padded, current + block, starts)

    padded = lax.fori_loop(0, TILES_X * TILES_Y, add_tile, padded)
    return padded[:, HALO:HALO + NX, HALO:HALO + NY]


def tridiagonal(lower, diag, upper, rhs):
    def forward(carry, row):
        prev_mod, prev_right = carry
        low_c, mid_c, up_c, right = row
        denom = mid_c - low_c * prev_mod
        next_mod = up_c / denom
        next_right = (right - low_c * prev_right) / denom
        return (next_mod, next_right), (next_mod, next_right)

    start = (jnp.zeros_like(diag[0]), jnp.zeros_like(rhs[0]))
    _, (mods, rights) = lax.scan(forward, start, (lower, diag, upper, rhs))

    def backward(later, row):
        mod_c, right = row
        value = right - mod_c * later
        return value, value

    _, values = lax.scan(backward, jnp.zeros_like(rhs[0]), (mods, rights), reverse=True)
    return values


def reference(u_wind, theta, act_points, point_count, klass, diff_table):
    force = project(act_points, point_count)
    columns = NX * NY
    kappa = jnp.take(diff_table.T, klass.reshape(columns).astype(jnp.int32), axis=1)
    levels = jnp.arange(NZ)[:, None]
    below = jnp.where(levels >= 1, kappa, jnp.zeros_like(kappa))
    above = jnp.concatenate([kappa[1:], jnp.zeros((1, columns), jnp.float32)], 0)
    scales = jnp.array([1.0, THETA_SCALE], jnp.float32)[None, :, None]
    lower = -scales * below[:, None, :]
    upper = -scales * above[:, None, :]
    diag = 1.0 + scales * (below + above)[:, None, :]
    rhs = jnp.stack([(u_wind + force).reshape(NZ, columns), theta.reshape(NZ, columns)], 1)
    values = tridiagonal(lower, diag, upper, rhs)
    return values[:, 0].reshape(NZ, NX, NY), values[:, 1].reshape(NZ, NX, NY)
```

```python
import functools
import math

import jax
import jax.numpy as jnp
from jax import lax
from jax.experimental import pallas as pl
from jax.experimental.pallas import tpu as pltpu
from jax.sharding import PartitionSpec as P

HALO = 16
THETA_SCALE = 1.25
CLASSES = 16
LANES = 128
STRAIGHT = ((-1, 0), (1, 0), (0, -1), (0, 1))
DIAGONAL = ((-1, -1), (1, 1), (1, -1), (-1, 1))
TILES = STRAIGHT + DIAGONAL
SPARE = len(TILES)
ACROSS = (2, 3, 4, 5, 6, 7)
NT = (((1,), (1,)), ((), ()))
VMEM_LIMIT = 48 * 1024 * 1024


def lane_iota(shape):
    return lax.broadcasted_iota(jnp.int32, shape, len(shape) - 1)


def gauss(coords, centres):
    offset = (coords - centres) * (2.0 / HALO * math.sqrt(math.log2(math.e)))
    return jnp.exp2(-(offset * offset))


def halves(value):
    high = value.astype(jnp.bfloat16)
    return high, (value - high.astype(jnp.float32)).astype(jnp.bfloat16)


def whole_blocks(live, size):
    return lax.div(live + (size - 1), size)


def pick(table_row, index):
    return jnp.take_along_axis(jnp.broadcast_to(table_row, index.shape), index, axis=1, mode="promise_in_bounds")


def pack_columns(full):
    tail = full[24:32]
    lane = lane_iota((8, LANES))
    parts = []
    for part in range(3):
        moved = pltpu.roll(tail, 96 - 32 * part, 1)
        parts.append(jnp.where(lane < 96, full[8 * part : 8 * part + 8], moved))
    return jnp.concatenate(parts, 0)


def unpack_columns(dense):
    lane = lane_iota((8, LANES))
    first = pltpu.roll(dense[0:8], 32, 1)
    second = pltpu.roll(dense[8:16], 64, 1)
    third = pltpu.roll(dense[16:24], 96, 1)
    tail = jnp.where(lane < 32, first, jnp.where(lane < 64, second, third))
    return jnp.concatenate([dense, tail], 0)


def widen(ref_value):
    rows, cols = ref_value.shape
    return jnp.concatenate([ref_value, jnp.zeros((rows, LANES - cols), ref_value.dtype)], 1)


def column_tables(depth, levels, slabs, table_ref, up_ref, down_ref, mix_ref, inv_ref, square_ref):
    slab = lax.axis_index("gz")
    inv_ref[...] = 1.0 / table_ref[...]
    value = jnp.ones((1, LANES), jnp.float32)
    flux = value
    high = value
    back = value
    up_ref[0:1, :] = value
    down_ref[depth - 1 : depth, :] = high
    for step in range(1, depth):
        value = value + flux * inv_ref[step : step + 1, :]
        flux = flux + value
        up_ref[step : step + 1, :] = value
        other = depth - 1 - step
        high = high + back * inv_ref[other + 1 : other + 2, :]
        back = back + high
        down_ref[other : other + 1, :] = high
    down_ref[...] = down_ref[...] * (1.0 / flux)
    level = lax.broadcasted_iota(jnp.int32, (depth, LANES), 0)
    lane = lane_iota((depth, LANES))
    below = jnp.where(level < slab * levels, up_ref[...], 0.0)
    above = jnp.where(level >= (slab + 1) * levels, down_ref[...], 0.0)
    mixed = jnp.where(lane < CLASSES, below, pltpu.roll(above, CLASSES, 1))
    square_ref[0:depth, :] = mixed
    square_ref[depth:LANES, :] = jnp.zeros((LANES - depth, LANES), jnp.float32)
    mix_ref[...] = jnp.transpose(square_ref[...])[0 : 2 * CLASSES, :]


def send_kernel(points_hbm, count_ref, out_ref, sem):
    points = pltpu.make_async_copy(points_hbm, out_ref.at[0:32], sem)
    points.start()
    out_ref[32:40, :] = count_ref[...].astype(jnp.float32)
    points.wait()


def own_kernel(slabs, u_hbm, theta_hbm, klass_hbm, table_ref, sent_ref,
               sums_ref, up_ref, down_ref, mix_ref, index_ref, acc_ref,
               inv_ref, square_ref, u_ref, theta_ref, klass_ref, sems):
    levels, rows, cols = u_ref.shape
    depth = levels * slabs
    slab = lax.axis_index("gz")
    copies = [
        pltpu.make_async_copy(source, target, sems.at[number])
        for number, (source, target) in enumerate(
            ((klass_hbm, klass_ref), (u_hbm, u_ref), (theta_hbm, theta_ref))
        )
    ]
    for copy in copies:
        copy.start()
    live = jnp.max(sent_ref[32:40, :]).astype(jnp.int32)
    column_tables(depth, levels, slabs, table_ref, up_ref, down_ref, mix_ref, inv_ref, square_ref)
    acc_ref[...] = jnp.zeros_like(acc_ref)
    mix = mix_ref[:, 0:depth]

    def chunk(c, carry):
        entries = [(0, 4 * c + k, live, 0, 0) for k in range(4)]
        add_points(sent_ref, entries, mix, acc_ref, 0, rows, False, cols)
        return carry

    lax.fori_loop(0, whole_blocks(live, 4 * LANES), chunk, 0)
    for copy in copies:
        copy.wait()
    index = widen(klass_ref[...])
    index_ref[...] = index
    zero = jnp.zeros(index.shape, jnp.float32)
    sums = [zero, zero, zero, zero]
    start = pl.multiple_of(slab * levels, levels)
    ups = up_ref[pl.ds(start, levels), :]
    downs = down_ref[pl.ds(start, levels), :]
    for z in range(levels):
        u_rows = widen(u_ref[z])
        t_rows = widen(theta_ref[z])
        sums[0] = sums[0] + pick(ups[z : z + 1], index) * u_rows
        sums[1] = sums[1] + pick(ups[z : z + 1], index + CLASSES) * t_rows
        sums[2] = sums[2] + pick(downs[z : z + 1], index) * u_rows
        sums[3] = sums[3] + pick(downs[z : z + 1], index + CLASSES) * t_rows
    for number, part in enumerate(sums):
        sums_ref[24 * number : 24 * number + 24, :] = pack_columns(part)


def pack_kernel(slabs, sums_ref, straight_ref, diagonal_ref, out_ref):
    slab = lax.axis_index("gz")
    counts = jnp.where(lane_iota((8, LANES)) < LANES // 2, straight_ref[32:40, :], diagonal_ref[32:40, :])
    for target in range(slabs):
        out_ref[target, 0:48, :] = jnp.where(target > slab, sums_ref[0:48, :], sums_ref[48:96, :])
        out_ref[target, 48:80, :] = straight_ref[0:32, :]
        out_ref[target, 80:112, :] = diagonal_ref[0:32, :]
        out_ref[target, 112:120, :] = counts


def heights(points_ref, entries, mix, levels):
    slab = lax.axis_index("gz")
    depth = mix.shape[1]
    places = []
    parts = []
    for base, which, live, _, _ in entries:
        px, py, pz, weight = (points_ref[pl.ds(base + 8 * a + which, 1), :] for a in range(4))
        weight = jnp.where(which * LANES + lane_iota((1, LANES)) < live, weight, 0.0)
        places.append((px, py, weight))
        z = lax.broadcasted_iota(jnp.int32, (depth, LANES), 0)
        own = slab * levels + lax.broadcasted_iota(jnp.int32, (levels, LANES), 0)
        parts.append((gauss(z.astype(jnp.float32), pz), gauss(own.astype(jnp.float32), pz)))
    gz, own = (jnp.concatenate(both, 1) for both in zip(*parts))
    other = jnp.dot(mix, gz, precision=lax.Precision.HIGHEST, preferred_element_type=jnp.float32)
    return places, jnp.concatenate([own, other], 0)


def add_points(points_ref, entries, mix, acc_ref, first_row, n_rows, masked, cols):
    deep, rows, _ = acc_ref.shape
    tile_x, tile_y = (lax.axis_index(name) for name in ("gx", "gy"))
    places, high = heights(points_ref, entries, mix, deep - 2 * CLASSES)
    i = tile_x * rows + first_row + lax.broadcasted_iota(jnp.int32, (n_rows, LANES), 0)
    j = tile_y * cols + lax.broadcasted_iota(jnp.int32, (cols, LANES), 0)
    parts = []
    for (px, py, weight), (_, _, _, at_x, _) in zip(places, entries):
        gi = gauss(i.astype(jnp.float32), px)
        if masked:
            inner = i - (at_x * rows - HALO)
            gi = jnp.where((inner >= 0) & (inner < rows + 2 * HALO), gi, 0.0)
        parts.append((gi, gauss(j.astype(jnp.float32), py) * weight))
    gi, gj = (jnp.concatenate(both, 1) for both in zip(*parts))
    width = gi.shape[1]
    right_high, right_low = halves(gj)
    gap = jnp.zeros((LANES - cols, width), jnp.bfloat16)
    right_high = jnp.concatenate([right_high, gap], 0)
    right = jnp.concatenate([right_high, right_low, gap], 0)
    block = 2 * LANES // n_rows
    for first in range(0, deep, block):
        left = (high[first : first + block, None, :] * gi[None]).reshape(block * n_rows, width)
        left_high, left_low = halves(left)
        wide = lax.dot_general(left_high, right, NT, preferred_element_type=jnp.float32)
        narrow = lax.dot_general(left_low, right_high, NT, preferred_element_type=jnp.float32)
        total = wide[:, :LANES] + wide[:, LANES:] + narrow
        acc_ref[first : first + block, first_row : first_row + n_rows, :] += total.reshape(block, n_rows, LANES)


def add_across(points_ref, entries, mix, side_ref, rows, cols):
    deep = side_ref.shape[0]
    tile_x, tile_y = (lax.axis_index(name) for name in ("gx", "gy"))
    places, high = heights(points_ref, entries, mix, deep - 2 * CLASSES)
    i = tile_x * rows + lax.broadcasted_iota(jnp.int32, (rows, LANES), 0)
    column = lax.broadcasted_iota(jnp.int32, (HALO, LANES), 0)
    parts = []
    for (px, py, weight), (_, _, _, at_x, at_y) in zip(places, entries):
        before = at_y < tile_y
        j = tile_y * cols + jnp.where(before, 0, cols - HALO) + column
        inner = i - (at_x * rows - HALO)
        gi = gauss(i.astype(jnp.float32), px)
        gi = jnp.where((inner >= 0) & (inner < rows + 2 * HALO), gi, 0.0)
        gi = jnp.concatenate([jnp.where(before, gi, 0.0), jnp.where(before, 0.0, gi)], 0)
        parts.append((gauss(j.astype(jnp.float32), py) * weight, gi))
    gj, gi = (jnp.concatenate(both, 1) for both in zip(*parts))
    width = gi.shape[1]
    right_high, right_low = halves(gi)
    right = jnp.concatenate([right_high, right_low], 0)
    right_high = jnp.concatenate([right_high, jnp.zeros_like(right_high)], 0)
    block = 2 * LANES // HALO
    for first in range(0, deep, block):
        left = (high[first : first + block, None, :] * gj[None]).reshape(block * HALO, width)
        left_high, left_low = halves(left)
        total = lax.dot_general(left_high, right, NT, preferred_element_type=jnp.float32)
        total = total + lax.dot_general(left_low, right_high, NT, preferred_element_type=jnp.float32)
        side_ref[first : first + block] += total.reshape(block, HALO, LANES)


def by_class(value_of, index):
    low = jnp.zeros(index.shape, jnp.float32)
    high = low
    for c in range(CLASSES):
        here = index == c
        low = jnp.where(here, value_of(c), low)
        high = jnp.where(here, value_of(CLASSES + c), high)
    return low, high


def side_fields(side_ref, index_ref, stack_ref, rows, cols):
    levels = side_ref.shape[0] - 2 * CLASSES
    square = jnp.concatenate([index_ref[...], jnp.zeros((LANES - rows, LANES), jnp.int32)], 0)
    square = jnp.transpose(square.astype(jnp.float32))
    first = square[0:HALO]
    last = pltpu.roll(square[cols - HALO : cols], rows, 1)
    index = jnp.where(lane_iota(first.shape) < rows, first, last).astype(jnp.int32)

    def folded(z):
        return side_ref[z] + pltpu.roll(side_ref[z], 2 * rows, 1)

    for z in range(levels):
        stack_ref[z * HALO : (z + 1) * HALO, :] = folded(z)
    low, high = by_class(lambda c: folded(levels + c), index)
    stack_ref[levels * HALO : (levels + 1) * HALO, :] = low
    stack_ref[(levels + 1) * HALO : (levels + 2) * HALO, :] = high
    lane = lane_iota((rows, LANES))
    fields = []
    per = LANES // HALO
    for group in range(stack_ref.shape[0] // LANES):
        turned = jnp.transpose(stack_ref[group * LANES : (group + 1) * LANES, :])
        for k in range(per):
            if group * per + k < levels + 2:
                before = pltpu.roll(turned[0:rows], (LANES - k * HALO) % LANES, 1)
                after = pltpu.roll(turned[rows : 2 * rows], (LANES + cols - HALO - k * HALO) % LANES, 1)
                fields.append(jnp.where(lane < HALO, before, jnp.where((lane >= cols - HALO) & (lane < cols), after, 0.0)))
    return fields


def solve_field(in_ref, index, ups, downs, low, high, force_of, out_ref, gather_ref, copy_of):
    levels, _, cols = in_ref.shape
    for z in range(levels):
        right = force_of(z, widen(in_ref[z]))
        up = pick(ups[z : z + 1], index)
        down = pick(downs[z : z + 1], index)
        low = low + up * right
        gather_ref[0, z] = down * low
        gather_ref[1, z] = up
        gather_ref[2, z] = down * right
    for z in range(levels - 1, -1, -1):
        out_ref[z] = (gather_ref[0, z] + gather_ref[1, z] * high)[:, :cols]
        high = high + gather_ref[2, z]
        if z == levels // 2:
            copy_of(1).start()
    copy_of(0).start()


def last_kernel(slabs, got_ref, own_ref, u_hbm, theta_hbm, index_ref, up_ref, down_ref, mix_ref, u_out, theta_out,
                acc_ref, points_ref, side_ref, stack_ref, gather_ref, u_ref, theta_ref, u_new, theta_new,
                live_ref, at_ref, list_ref, sems, out_sems):
    levels, rows, cols = u_ref.shape
    copies = [
        pltpu.make_async_copy(theta_hbm, theta_ref, sems.at[0]),
        pltpu.make_async_copy(u_hbm, u_ref, sems.at[1]),
    ]
    for copy in copies:
        copy.start()

    def out_copy(field, half):
        source, target = ((u_new, u_out), (theta_new, theta_out))[field]
        part = pl.ds(half * (levels // 2), levels // 2)
        return pltpu.make_async_copy(source.at[part], target.at[part], out_sems.at[field, half])

    tile_x, tile_y, slab = (lax.axis_index(name) for name in ("gx", "gy", "gz"))
    depth = levels * slabs
    mix = mix_ref[:, 0:depth]
    lane8 = lane_iota((8, LANES))
    low_sum = jnp.zeros((48, LANES), jnp.float32)
    high_sum = low_sum
    for source in range(slabs):
        points_ref[source * 32 : source * 32 + 32, :] = got_ref[source, 48:80, :]
        points_ref[(source + slabs) * 32 : (source + slabs) * 32 + 32, :] = got_ref[source, 80:112, :]
        counts = got_ref[source, 112:120, :]
        live_ref[source] = jnp.max(jnp.where(lane8 < LANES // 2, counts, 0.0)).astype(jnp.int32)
        live_ref[source + slabs] = jnp.max(jnp.where(lane8 < LANES // 2, 0.0, counts)).astype(jnp.int32)
        edge = got_ref[source, 0:48, :]
        low_sum = low_sum + jnp.where(source < slab, edge, 0.0)
        high_sum = high_sum + jnp.where(source > slab, edge, 0.0)
    points_ref[SPARE * 32 : SPARE * 32 + 32, :] = jnp.zeros((32, LANES), jnp.float32)
    live_ref[SPARE] = 0
    for number, (dx, dy) in enumerate(TILES + ((0, 1),)):
        at_ref[2 * number] = tile_x + dx
        at_ref[2 * number + 1] = tile_y + dy

    index = index_ref[...]
    start = pl.multiple_of(slab * levels, levels)
    ups = up_ref[pl.ds(start, levels), :]
    downs = down_ref[pl.ds(start, levels), :]
    copies[0].wait()
    solve_field(theta_ref, index + CLASSES, ups, downs, unpack_columns(low_sum[24:48]), unpack_columns(high_sum[24:48]),
                lambda z, right: right, theta_new, gather_ref, functools.partial(out_copy, 1))

    acc_ref[...] = own_ref[...]
    for number, first_row in ((0, 0), (1, rows - HALO)):
        live = live_ref[number]

        def chunk(c, carry):
            entries = [(number * 32, 2 * c + k, live, at_ref[2 * number], at_ref[2 * number + 1]) for k in range(2)]
            add_points(points_ref, entries, mix, acc_ref, first_row, HALO, True, cols)
            return carry

        lax.fori_loop(0, whole_blocks(live, 2 * LANES), chunk, 0)

    filled = jnp.int32(0)
    for number in ACROSS:
        def note(k, carry):
            list_ref[filled + k] = number * 8 + k
            return carry

        blocks = whole_blocks(live_ref[number], LANES)
        lax.fori_loop(0, blocks, note, 0)
        filled = filled + blocks
    list_ref[filled] = SPARE * 8
    side_ref[...] = jnp.zeros_like(side_ref)
    stack_ref[...] = jnp.zeros_like(stack_ref)

    def pair(c, carry):
        entries = []
        for k in range(2):
            entry = list_ref[2 * c + k]
            number = lax.shift_right_logical(entry, 3)
            entries.append((number * 32, lax.bitwise_and(entry, 7), live_ref[number], at_ref[2 * number],
                            at_ref[2 * number + 1]))
        add_across(points_ref, entries, mix, side_ref, rows, cols)
        return carry

    lax.fori_loop(0, whole_blocks(filled, 2), pair, 0)
    fields = side_fields(side_ref, index_ref, stack_ref, rows, cols)
    low_force, high_force = by_class(lambda c: acc_ref[levels + c], index)
    copies[1].wait()
    solve_field(u_ref, index, ups, downs,
                unpack_columns(low_sum[0:24]) + low_force + fields[levels],
                unpack_columns(high_sum[0:24]) + high_force + fields[levels + 1],
                lambda z, right: right + acc_ref[z] + fields[z], u_new, gather_ref, functools.partial(out_copy, 0))
    for field in range(2):
        for half in range(2):
            out_copy(field, half).wait()


def lateral(offsets, tiles_x, tiles_y, slabs):
    pairs = []
    for x in range(tiles_x):
        for y in range(tiles_y):
            for t in range(slabs):
                sx, sy = x + offsets[t][0], y + offsets[t][1]
                if 0 <= sx < tiles_x and 0 <= sy < tiles_y:
                    pairs.append(((sx * tiles_y + sy) * slabs + t, (x * tiles_y + y) * slabs + t))
    return pairs


def shards(u_wind, theta, act_points, point_count, klass, diff_table):
    levels, rows, cols = u_wind.shape
    tiles_x, tiles_y, slabs = (lax.axis_size(name) for name in ("gx", "gy", "gz"))
    depth = levels * slabs
    f32 = jnp.float32
    stay = lambda x: pltpu.with_memory_space_constraint(x, pltpu.HBM)
    u_wind, theta, klass = stay(u_wind), stay(theta), stay(klass)
    vmem = pl.BlockSpec(memory_space=pltpu.VMEM)
    hbm = pl.BlockSpec(memory_space=pltpu.HBM)
    params = pltpu.CompilerParams(vmem_limit_bytes=VMEM_LIMIT)
    sent = pl.pallas_call(
        send_kernel,
        out_shape=jax.ShapeDtypeStruct((40, LANES), f32),
        in_specs=[hbm, vmem],
        out_specs=vmem,
        scratch_shapes=[pltpu.SemaphoreType.DMA],
        compiler_params=params,
        name="send",
    )(stay(act_points.reshape(32, LANES)), jnp.broadcast_to(point_count, (8, LANES)))
    axes = ("gx", "gy", "gz")
    straight = lax.ppermute(sent, axes, lateral(STRAIGHT, tiles_x, tiles_y, slabs))
    diagonal = lax.ppermute(sent, axes, lateral(DIAGONAL, tiles_x, tiles_y, slabs))
    table = diff_table.T
    table = jnp.concatenate([table, THETA_SCALE * table, jnp.ones((depth, LANES - 2 * CLASSES), f32)], 1)
    acc_shape = (levels + 2 * CLASSES, rows, LANES)
    field = pltpu.VMEM(u_wind.shape, f32)
    sums, ups, downs, mix, index, own = pl.pallas_call(
        functools.partial(own_kernel, slabs),
        out_shape=[
            jax.ShapeDtypeStruct((96, LANES), f32),
            jax.ShapeDtypeStruct((depth, LANES), f32),
            jax.ShapeDtypeStruct((depth, LANES), f32),
            jax.ShapeDtypeStruct((2 * CLASSES, LANES), f32),
            jax.ShapeDtypeStruct((rows, LANES), jnp.int32),
            jax.ShapeDtypeStruct(acc_shape, f32),
        ],
        in_specs=[hbm, hbm, hbm, vmem, vmem],
        out_specs=[vmem] * 6,
        scratch_shapes=[
            pltpu.VMEM((depth, LANES), f32),
            pltpu.VMEM((LANES, LANES), f32),
            field,
            field,
            pltpu.VMEM((rows, cols), jnp.int32),
            pltpu.SemaphoreType.DMA((3,)),
        ],
        compiler_params=params,
        cost_estimate=pl.CostEstimate(flops=2 * 10**9, bytes_accessed=10**6, transcendentals=10**5),
        name="own_tile",
    )(u_wind, theta, klass, table, sent)
    packed = pl.pallas_call(
        functools.partial(pack_kernel, slabs),
        out_shape=jax.ShapeDtypeStruct((slabs, 120, LANES), f32),
        compiler_params=params,
        name="pack",
    )(sums, straight, diagonal)
    got = lax.all_to_all(packed, "gz", 0, 0)
    return pl.pallas_call(
        functools.partial(last_kernel, slabs),
        out_shape=[jax.ShapeDtypeStruct(u_wind.shape, f32)] * 2,
        in_specs=[vmem, vmem, hbm, hbm, vmem, vmem, vmem, vmem],
        out_specs=[hbm] * 2,
        scratch_shapes=[
            pltpu.VMEM(acc_shape, f32),
            pltpu.VMEM(((SPARE + 1) * 32, LANES), f32),
            pltpu.VMEM((levels + 2 * CLASSES, HALO, LANES), f32),
            pltpu.VMEM((3 * LANES, LANES), f32),
            pltpu.VMEM((3, levels, rows, LANES), f32),
            field,
            field,
            field,
            field,
            pltpu.SMEM((SPARE + 1,), jnp.int32),
            pltpu.SMEM((2 * SPARE + 2,), jnp.int32),
            pltpu.SMEM((8 * SPARE,), jnp.int32),
            pltpu.SemaphoreType.DMA((2,)),
            pltpu.SemaphoreType.DMA((2, 2)),
        ],
        compiler_params=params,
        name="solve",
    )(got, own, u_wind, theta, index, ups, downs, mix)


def solution(mesh):
    return jax.shard_map(
        shards,
        mesh=mesh,
        in_specs=(
            P("gz", "gx", "gy"),
            P("gz", "gx", "gy"),
            P(None, "gx", "gy", None),
            P("gx", "gy"),
            P("gx", "gy"),
            P(),
        ),
        out_specs=(P("gz", "gx", "gy"), P("gz", "gx", "gy")),
        check_vma=False,
    )
```

```python
import functools
import math

import jax
import jax.numpy as jnp
from jax import lax
from jax.experimental import pallas as pl
from jax.experimental.pallas import tpu as pltpu
from jax.sharding import PartitionSpec as P

HALO = 16
THETA_SCALE = 1.25
CLASSES = 16
LANES = 128
STRAIGHT = ((-1, 0), (1, 0), (0, -1), (0, 1))
DIAGONAL = ((-1, -1), (1, 1), (1, -1), (-1, 1))
TILES = STRAIGHT + DIAGONAL
SPARE = len(TILES)
PIECES = 4
FINE = HALO // 2
LOG2E = math.log2(math.e)
MANY = 8
ACROSS = (2, 3, 4, 5, 6, 7)
NT = (((1,), (1,)), ((), ()))
VMEM_LIMIT = 48 * 1024 * 1024


def lane_iota(shape):
    return lax.broadcasted_iota(jnp.int32, shape, len(shape) - 1)


def gauss(coords, centres):
    offset = (coords - centres) * (2.0 / HALO * math.sqrt(LOG2E))
    return jnp.exp2(-(offset * offset))


def halves(value):
    high = value.astype(jnp.bfloat16)
    return high, (value - high.astype(jnp.float32)).astype(jnp.bfloat16)


def mix_halves(mix_ref, depth):
    high, low = halves(mix_ref[...])
    low = pltpu.roll(low.astype(jnp.float32), depth, 1)
    both = jnp.where(lane_iota(low.shape) < depth, high.astype(jnp.float32), low).astype(jnp.bfloat16)
    return jnp.concatenate([both, high[:, :depth]], 1)


def whole_blocks(live, size):
    return lax.div(live + (size - 1), size)


def in_batches(blocks, add):
    done = jnp.int32(0)
    for size in (MANY, MANY // 2, MANY // 4):
        spare = size // 2 - 1 if size > MANY // 4 else size - 1
        steps = lax.div(blocks - done + spare, size)

        def batch(c, carry, done=done, size=size):
            add(done + size * c, size)
            return carry

        lax.fori_loop(0, steps, batch, 0)
        done = jnp.minimum(done + size * steps, blocks)


def pick(table_row, index):
    return jnp.take_along_axis(jnp.broadcast_to(table_row, index.shape), index, axis=1, mode="promise_in_bounds")


def pack_columns(full):
    tail = full[24:32]
    lane = lane_iota((8, LANES))
    parts = []
    for part in range(3):
        moved = pltpu.roll(tail, 96 - 32 * part, 1)
        parts.append(jnp.where(lane < 96, full[8 * part : 8 * part + 8], moved))
    return jnp.concatenate(parts, 0)


def unpack_columns(dense):
    lane = lane_iota((8, LANES))
    first = pltpu.roll(dense[0:8], 32, 1)
    second = pltpu.roll(dense[8:16], 64, 1)
    third = pltpu.roll(dense[16:24], 96, 1)
    tail = jnp.where(lane < 32, first, jnp.where(lane < 64, second, third))
    return jnp.concatenate([dense, tail], 0)


def widen(ref_value):
    rows, cols = ref_value.shape
    return jnp.concatenate([ref_value, jnp.zeros((rows, LANES - cols), ref_value.dtype)], 1)


def column_tables(depth, levels, slabs, table_ref, up_ref, down_ref, mix_ref, inv_ref, square_ref):
    slab = lax.axis_index("gz")
    square_ref[...] = jnp.ones((LANES, LANES), jnp.float32)
    square_ref[0:CLASSES, 0:depth] = table_ref[...]
    square_ref[CLASSES : 2 * CLASSES, 0:depth] = THETA_SCALE * table_ref[...]
    inv_ref[...] = 1.0 / jnp.transpose(square_ref[...])[0:depth]
    value = jnp.ones((1, LANES), jnp.float32)
    flux = value
    high = value
    back = value
    up_ref[0:1, :] = value
    down_ref[depth - 1 : depth, :] = high
    for step in range(1, depth):
        value = value + flux * inv_ref[step : step + 1, :]
        flux = flux + value
        up_ref[step : step + 1, :] = value
        other = depth - 1 - step
        high = high + back * inv_ref[other + 1 : other + 2, :]
        back = back + high
        down_ref[other : other + 1, :] = high
    down_ref[...] = down_ref[...] * (1.0 / flux)
    level = lax.broadcasted_iota(jnp.int32, (depth, LANES), 0)
    lane = lane_iota((depth, LANES))
    below = jnp.where(level < slab * levels, up_ref[...], 0.0)
    above = jnp.where(level >= (slab + 1) * levels, down_ref[...], 0.0)
    mixed = jnp.where(lane < CLASSES, below, pltpu.roll(above, CLASSES, 1))
    square_ref[0:depth, :] = mixed
    square_ref[depth:LANES, :] = jnp.zeros((LANES - depth, LANES), jnp.float32)
    mix_ref[...] = jnp.transpose(square_ref[...])[0 : 2 * CLASSES, :]


def own_kernel(slabs, u_hbm, theta_hbm, klass_hbm, table_ref, sent_ref,
               sums_ref, mix_ref, index_ref, acc_ref, u_ref, theta_ref, picks_ref,
               up_ref, down_ref, inv_ref, square_ref, klass_ref, sems):
    levels, rows, cols = u_ref.shape
    depth = levels * slabs
    slab = lax.axis_index("gz")
    part = levels // PIECES
    copies = [pltpu.make_async_copy(klass_hbm, klass_ref, sems.at[0])]
    for piece in range(PIECES):
        at = pl.ds(piece * part, part)
        copies.append(pltpu.make_async_copy(u_hbm.at[at], u_ref.at[at], sems.at[1 + 2 * piece]))
        copies.append(pltpu.make_async_copy(theta_hbm.at[at], theta_ref.at[at], sems.at[2 + 2 * piece]))
    for copy in copies:
        copy.start()
    live = jnp.max(sent_ref[32:40, :]).astype(jnp.int32)
    column_tables(depth, levels, slabs, table_ref, up_ref, down_ref, mix_ref, inv_ref, square_ref)
    acc_ref[...] = jnp.zeros_like(acc_ref)
    mix = mix_halves(mix_ref, depth)

    def add(first, n):
        entries = [(0, first + k, live, 0, 0) for k in range(n)]
        add_points(sent_ref, entries, mix, acc_ref, tuple(range(rows // FINE)), cols)

    in_batches(whole_blocks(live, LANES), add)
    copies[0].wait()
    index = widen(klass_ref[...])
    index_ref[...] = index
    zero = jnp.zeros(index.shape, jnp.float32)
    start = pl.multiple_of(slab * levels, levels)
    ups = up_ref[pl.ds(start, levels), :]
    downs = down_ref[pl.ds(start, levels), :]
    for z in range(levels):
        picks_ref[0, z] = pick(ups[z : z + 1], index)
        picks_ref[1, z] = pick(ups[z : z + 1], index + CLASSES)
        picks_ref[2, z] = pick(downs[z : z + 1], index)
        picks_ref[3, z] = pick(downs[z : z + 1], index + CLASSES)
    sums = [zero, zero, zero, zero]
    for copy in copies[1:]:
        copy.wait()
    for z in range(levels):
        u_rows = widen(u_ref[z])
        t_rows = widen(theta_ref[z])
        sums[0] = sums[0] + picks_ref[0, z] * u_rows
        sums[1] = sums[1] + picks_ref[1, z] * t_rows
        sums[2] = sums[2] + picks_ref[2, z] * u_rows
        sums[3] = sums[3] + picks_ref[3, z] * t_rows
    for number, part in enumerate(sums):
        sums_ref[24 * number : 24 * number + 24, :] = pack_columns(part)


def pack_kernel(slabs, sums_ref, straight_ref, diagonal_ref, out_ref):
    slab = lax.axis_index("gz")
    counts = straight_ref[32:40, :] + pltpu.roll(diagonal_ref[32:40, :], LANES // 2, 1)
    for target in range(slabs):
        out_ref[target, 0:48, :] = jnp.where(target > slab, sums_ref[0:48, :], sums_ref[48:96, :])
        out_ref[target, 48:80, :] = straight_ref[0:32, :]
        out_ref[target, 80:112, :] = diagonal_ref[0:32, :]
        out_ref[target, 112:120, :] = counts


def heights(points_ref, entries, mix, levels):
    slab = lax.axis_index("gz")
    depth = mix.shape[1] // 3
    places = []
    parts = []
    for base, which, live, _, _ in entries:
        px, py, pz, weight = (points_ref[pl.ds(base + 8 * a + which, 1), :] for a in range(4))
        alive = which * LANES + lane_iota((1, LANES)) < live
        places.append((px, py, jnp.where(alive, weight, 0.0), alive))
        z = lax.broadcasted_iota(jnp.int32, (depth, LANES), 0)
        own = slab * levels + lax.broadcasted_iota(jnp.int32, (levels, LANES), 0)
        parts.append((gauss(z.astype(jnp.float32), pz), gauss(own.astype(jnp.float32), pz)))
    gz, own = (jnp.concatenate(both, 1) for both in zip(*parts))
    gz_high, gz_low = halves(gz)
    other = jnp.dot(mix, jnp.concatenate([gz_high, gz_high, gz_low], 0), preferred_element_type=jnp.float32)
    return places, jnp.concatenate([own, other], 0)


def left_halves(high, fine):
    deep, width = high.shape
    return halves((high[:, None, :] * fine[None]).reshape(deep * FINE, width))


def fine_and_coarse(place, steps):
    cell = lax.broadcasted_iota(jnp.int32, (FINE,) + place.shape[1:], 0).astype(jnp.float32)
    fine = gauss(cell, place)
    coarse = [jnp.exp2(LOG2E * (2.0 * step / FINE * place - float(step * step))) for step in steps]
    return fine, coarse


def add_points(points_ref, entries, mix, acc_ref, steps, cols):
    deep, rows, _ = acc_ref.shape
    tile_x, tile_y = (lax.axis_index(name) for name in ("gx", "gy"))
    places, high = heights(points_ref, entries, mix, deep - 2 * CLASSES)
    j = lax.broadcasted_iota(jnp.int32, (cols, LANES), 0).astype(jnp.float32)
    parts = []
    for px, py, weight, alive in places:
        x = jnp.where(alive, px - (tile_x * rows).astype(jnp.float32), 0.0)
        fine, coarse = fine_and_coarse(x, steps)
        gj = gauss(j, py - (tile_y * cols).astype(jnp.float32))
        parts.append([fine, gj] + [factor * weight for factor in coarse])
    fine, gj, *coarse = (jnp.concatenate(both, 1) for both in zip(*parts))
    gap = jnp.zeros((LANES - cols, gj.shape[1]), jnp.bfloat16)
    pairs = [halves(gj * factor) for factor in coarse]
    right_high = jnp.concatenate([x for pair in pairs for x in (pair[0], gap)], 0)
    right_low = jnp.concatenate([x for pair in pairs for x in (pair[1], gap)], 0)
    left_high, left_low = left_halves(high, fine)
    left = jnp.concatenate([left_high, left_low, left_high], 1)
    right = jnp.concatenate([right_high, right_high, right_low], 1)
    total = lax.dot_general(left, right, NT, preferred_element_type=jnp.float32)
    for number, step in enumerate(steps):
        part = total[:, number * LANES : (number + 1) * LANES].reshape(deep, FINE, LANES)
        acc_ref[:, step * FINE : (step + 1) * FINE, :] += part


def add_sides(points_ref, entries, mix, side_ref, rows, cols):
    deep = side_ref.shape[0]
    tile_x, tile_y = (lax.axis_index(name) for name in ("gx", "gy"))
    places, high = heights(points_ref, entries, mix, deep - 2 * CLASSES)
    i = lax.broadcasted_iota(jnp.int32, (rows, LANES), 0)
    parts = []
    for (px, py, weight, alive), (_, _, _, at_x, at_y) in zip(places, entries):
        before = at_y < tile_y
        y = py - (tile_y * cols).astype(jnp.float32)
        y = jnp.where(alive, jnp.where(before, y, float(cols - 1) - y), 0.0)
        fine, coarse = fine_and_coarse(y, (0, 1))
        backward = gauss(float(FINE - 1) - lax.broadcasted_iota(jnp.int32, fine.shape, 0).astype(jnp.float32), y)
        inner = i - ((at_x - tile_x) * rows - HALO)
        gi = gauss(i.astype(jnp.float32), px - (tile_x * rows).astype(jnp.float32)) * weight
        gi = jnp.where((inner >= 0) & (inner < rows + 2 * HALO), gi, 0.0)
        gi = jnp.concatenate([jnp.where(before, gi, 0.0), jnp.where(before, 0.0, gi)], 0)
        parts.append((jnp.where(before, fine, backward), gi, coarse[0], coarse[1]))
    fine, gi, *coarse = (jnp.concatenate(both, 1) for both in zip(*parts))
    right_high, right_low = halves(jnp.concatenate([gi * factor for factor in coarse], 0))
    right = jnp.concatenate(
        [jnp.concatenate([right_high, right_low], 0), jnp.concatenate([right_high, jnp.zeros_like(right_low)], 0)], 1
    )
    left = jnp.concatenate(left_halves(high, fine), 1)
    total = lax.dot_general(left, right, NT, preferred_element_type=jnp.float32)
    side_ref[...] += (total[:, :LANES] + total[:, LANES:]).reshape(side_ref.shape)


def cross_factor(step, cell):
    return jnp.exp2((-2.0 * LOG2E / FINE) * (step * cell).astype(jnp.float32))


def by_class(value_of, index):
    low = jnp.zeros(index.shape, jnp.float32)
    high = low
    for c in range(CLASSES):
        here = index == c
        low = jnp.where(here, value_of(c), low)
        high = jnp.where(here, value_of(CLASSES + c), high)
    return low, high


def side_fields(side_ref, index_ref, stack_ref, rows, cols):
    levels = side_ref.shape[0] - 2 * CLASSES
    square = jnp.concatenate([index_ref[...], jnp.zeros((LANES - rows, LANES), jnp.int32)], 0)
    square = jnp.transpose(square.astype(jnp.float32))
    first = square[0:HALO]
    last = pltpu.roll(square[cols - HALO : cols], rows, 1)
    index = jnp.where(lane_iota(first.shape) < rows, first, last).astype(jnp.int32)

    lane = lane_iota((FINE, LANES))
    line = lax.broadcasted_iota(jnp.int32, (FINE, LANES), 0)
    on_first = lane % (2 * rows) < rows
    cross = cross_factor(lane // (2 * rows), jnp.where(on_first, line, FINE - 1 - line))

    def folded(z):
        near = side_ref[z] * cross
        far = pltpu.roll(near, 2 * rows, 1)
        return jnp.concatenate([jnp.where(lane < rows, near, far), jnp.where(lane < rows, far, near)], 0)

    for z in range(levels):
        stack_ref[z * HALO : (z + 1) * HALO, :] = folded(z)
    low, high = by_class(lambda c: folded(levels + c), index)
    stack_ref[levels * HALO : (levels + 1) * HALO, :] = low
    stack_ref[(levels + 1) * HALO : (levels + 2) * HALO, :] = high
    wide = lane_iota((rows, LANES))
    fields = []
    per = LANES // HALO
    for group in range(stack_ref.shape[0] // LANES):
        turned = jnp.transpose(stack_ref[group * LANES : (group + 1) * LANES, :])
        for k in range(per):
            if group * per + k < levels + 2:
                before = pltpu.roll(turned[0:rows], (LANES - k * HALO) % LANES, 1)
                after = pltpu.roll(turned[rows : 2 * rows], (LANES + cols - HALO - k * HALO) % LANES, 1)
                fields.append(jnp.where(wide < HALO, before, jnp.where((wide >= cols - HALO) & (wide < cols), after, 0.0)))
    return fields


def solve_field(in_ref, picks_ref, field, low, high, force_of, out_ref, gather_ref, copy_of):
    levels, _, cols = in_ref.shape
    for z in range(levels):
        right = force_of(z, widen(in_ref[z]))
        down = picks_ref[2 + field, z]
        low = low + picks_ref[field, z] * right
        gather_ref[0, z] = down * low
        gather_ref[1, z] = down * right
    for z in range(levels - 1, -1, -1):
        out_ref[z] = (gather_ref[0, z] + picks_ref[field, z] * high)[:, :cols]
        high = high + gather_ref[1, z]
        if z % (levels // PIECES) == 0:
            copy_of(z // (levels // PIECES)).start()


def last_kernel(slabs, got_ref, own_ref, u_ref, theta_ref, index_ref, picks_ref, mix_ref, u_out, theta_out,
                acc_ref, points_ref, side_ref, stack_ref, gather_ref, u_new, theta_new,
                live_ref, at_ref, list_ref, out_sems):
    levels, rows, cols = u_ref.shape

    def out_copy(field, piece):
        source, target = ((u_new, u_out), (theta_new, theta_out))[field]
        part = pl.ds(piece * (levels // PIECES), levels // PIECES)
        return pltpu.make_async_copy(source.at[part], target.at[part], out_sems.at[field, piece])

    tile_x, tile_y, slab = (lax.axis_index(name) for name in ("gx", "gy", "gz"))
    depth = levels * slabs
    mix = mix_halves(mix_ref, depth)
    lane8 = lane_iota((8, LANES))
    low_sum = jnp.zeros((48, LANES), jnp.float32)
    high_sum = low_sum
    for source in range(slabs):
        points_ref[source * 32 : source * 32 + 32, :] = got_ref[source, 48:80, :]
        points_ref[(source + slabs) * 32 : (source + slabs) * 32 + 32, :] = got_ref[source, 80:112, :]
        counts = got_ref[source, 112:120, :]
        live_ref[source] = jnp.max(jnp.where(lane8 < LANES // 2, counts, 0.0)).astype(jnp.int32)
        live_ref[source + slabs] = jnp.max(jnp.where(lane8 < LANES // 2, 0.0, counts)).astype(jnp.int32)
        edge = got_ref[source, 0:48, :]
        low_sum = low_sum + jnp.where(source < slab, edge, 0.0)
        high_sum = high_sum + jnp.where(source > slab, edge, 0.0)
    points_ref[SPARE * 32 : SPARE * 32 + 32, :] = jnp.zeros((32, LANES), jnp.float32)
    live_ref[SPARE] = 0
    for number, (dx, dy) in enumerate(TILES + ((0, 1),)):
        at_ref[2 * number] = tile_x + dx
        at_ref[2 * number + 1] = tile_y + dy

    index = index_ref[...]
    solve_field(theta_ref, picks_ref, 1, unpack_columns(low_sum[24:48]), unpack_columns(high_sum[24:48]),
                lambda z, right: right, theta_new, gather_ref, functools.partial(out_copy, 1))

    acc_ref[...] = own_ref[...]
    for number, steps in ((0, (0, 1)), (1, (rows // FINE - 2, rows // FINE - 1))):
        live = live_ref[number]

        def add(first, n):
            entries = [(number * 32, first + k, live, 0, 0) for k in range(n)]
            add_points(points_ref, entries, mix, acc_ref, steps, cols)

        in_batches(whole_blocks(live, LANES), add)

    filled = jnp.int32(0)
    for number in ACROSS:
        for k in range(8):
            list_ref[filled + k] = number * 8 + k
        filled = filled + whole_blocks(live_ref[number], LANES)
    for k in range(MANY):
        list_ref[filled + k] = SPARE * 8
    side_ref[...] = jnp.zeros_like(side_ref)
    stack_ref[...] = jnp.zeros_like(stack_ref)

    def add_side(first, n):
        entries = []
        for k in range(n):
            entry = list_ref[first + k]
            number = lax.shift_right_logical(entry, 3)
            entries.append((number * 32, lax.bitwise_and(entry, 7), live_ref[number], at_ref[2 * number],
                            at_ref[2 * number + 1]))
        add_sides(points_ref, entries, mix, side_ref, rows, cols)

    in_batches(filled, add_side)
    fields = side_fields(side_ref, index_ref, stack_ref, rows, cols)
    row = lax.broadcasted_iota(jnp.int32, (rows, LANES), 0)
    cross = cross_factor(row // FINE, row % FINE)
    low_force, high_force = by_class(lambda c: acc_ref[levels + c], index)
    solve_field(u_ref, picks_ref, 0,
                unpack_columns(low_sum[0:24]) + low_force * cross + fields[levels],
                unpack_columns(high_sum[0:24]) + high_force * cross + fields[levels + 1],
                lambda z, right: right + acc_ref[z] * cross + fields[z], u_new, gather_ref, functools.partial(out_copy, 0))
    for field in range(2):
        for piece in range(PIECES):
            out_copy(field, piece).wait()


def lateral(offsets, tiles_x, tiles_y, slabs):
    pairs = []
    for x in range(tiles_x):
        for y in range(tiles_y):
            for t in range(slabs):
                sx, sy = x + offsets[t][0], y + offsets[t][1]
                if 0 <= sx < tiles_x and 0 <= sy < tiles_y:
                    pairs.append(((sx * tiles_y + sy) * slabs + t, (x * tiles_y + y) * slabs + t))
    return pairs


def shards(u_wind, theta, act_points, point_count, klass, diff_table):
    levels, rows, cols = u_wind.shape
    tiles_x, tiles_y, slabs = (lax.axis_size(name) for name in ("gx", "gy", "gz"))
    depth = levels * slabs
    f32 = jnp.float32
    stay = lambda x: pltpu.with_memory_space_constraint(x, pltpu.HBM)
    u_wind, theta, klass = stay(u_wind), stay(theta), stay(klass)
    vmem = pl.BlockSpec(memory_space=pltpu.VMEM)
    hbm = pl.BlockSpec(memory_space=pltpu.HBM)
    params = pltpu.CompilerParams(vmem_limit_bytes=VMEM_LIMIT)
    count = jnp.pad(point_count.astype(f32), ((0, 7), (0, LANES - 1)))
    sent = jnp.concatenate([act_points.reshape(32, LANES), count], 0)
    axes = ("gx", "gy", "gz")
    straight = lax.ppermute(sent, axes, lateral(STRAIGHT, tiles_x, tiles_y, slabs))
    diagonal = lax.ppermute(sent, axes, lateral(DIAGONAL, tiles_x, tiles_y, slabs))
    acc_shape = (levels + 2 * CLASSES, rows, LANES)
    field = pltpu.VMEM(u_wind.shape, f32)
    sums, mix, index, own, u_here, theta_here, picks = pl.pallas_call(
        functools.partial(own_kernel, slabs),
        out_shape=[
            jax.ShapeDtypeStruct((96, LANES), f32),
            jax.ShapeDtypeStruct((2 * CLASSES, LANES), f32),
            jax.ShapeDtypeStruct((rows, LANES), jnp.int32),
            jax.ShapeDtypeStruct(acc_shape, f32),
            jax.ShapeDtypeStruct(u_wind.shape, f32),
            jax.ShapeDtypeStruct(u_wind.shape, f32),
            jax.ShapeDtypeStruct((4, levels, rows, LANES), f32),
        ],
        in_specs=[hbm, hbm, hbm, vmem, vmem],
        out_specs=[vmem] * 7,
        scratch_shapes=[
            pltpu.VMEM((depth, LANES), f32),
            pltpu.VMEM((depth, LANES), f32),
            pltpu.VMEM((depth, LANES), f32),
            pltpu.VMEM((LANES, LANES), f32),
            pltpu.VMEM((rows, cols), jnp.int32),
            pltpu.SemaphoreType.DMA((1 + 2 * PIECES,)),
        ],
        compiler_params=params,
        cost_estimate=pl.CostEstimate(flops=2 * 10**9, bytes_accessed=10**6, transcendentals=10**5),
        name="own_tile",
    )(u_wind, theta, klass, diff_table, sent)
    packed = pl.pallas_call(
        functools.partial(pack_kernel, slabs),
        out_shape=jax.ShapeDtypeStruct((slabs, 120, LANES), f32),
        compiler_params=params,
        name="pack",
    )(sums, straight, diagonal)
    got = lax.all_to_all(packed, "gz", 0, 0)
    return pl.pallas_call(
        functools.partial(last_kernel, slabs),
        out_shape=[jax.ShapeDtypeStruct(u_wind.shape, f32)] * 2,
        in_specs=[vmem] * 7,
        out_specs=[hbm] * 2,
        scratch_shapes=[
            pltpu.VMEM(acc_shape, f32),
            pltpu.VMEM(((SPARE + 1) * 32, LANES), f32),
            pltpu.VMEM((levels + 2 * CLASSES, FINE, LANES), f32),
            pltpu.VMEM((3 * LANES, LANES), f32),
            pltpu.VMEM((2, levels, rows, LANES), f32),
            field,
            field,
            pltpu.SMEM((SPARE + 1,), jnp.int32),
            pltpu.SMEM((2 * SPARE + 2,), jnp.int32),
            pltpu.SMEM((8 * SPARE,), jnp.int32),
            pltpu.SemaphoreType.DMA((2, PIECES)),
        ],
        compiler_params=params,
        name="solve",
    )(got, own, u_here, theta_here, index, picks, mix)


def solution(mesh):
    return jax.shard_map(
        shards,
        mesh=mesh,
        in_specs=(
            P("gz", "gx", "gy"),
            P("gz", "gx", "gy"),
            P(None, "gx", "gy", None),
            P("gx", "gy"),
            P("gx", "gy"),
            P(),
        ),
        out_specs=(P("gz", "gx", "gy"), P("gz", "gx", "gy")),
        check_vma=False,
    )
```

```python
import functools
import math

import jax
import jax.numpy as jnp
from jax import lax
from jax.experimental import pallas as pl
from jax.experimental.pallas import tpu as pltpu
from jax.sharding import PartitionSpec as P

HALO = 16
THETA_SCALE = 1.25
CLASSES = 16
LANES = 128
STRAIGHT = ((-1, 0), (1, 0), (0, -1), (0, 1))
DIAGONAL = ((-1, -1), (1, 1), (1, -1), (-1, 1))
TILES = STRAIGHT + DIAGONAL
SPARE = len(TILES)
PIECES = 4
FINE = HALO // 2
LOG2E = math.log2(math.e)
MANY = 8
ACROSS = (2, 3, 4, 5, 6, 7)
NT = (((1,), (1,)), ((), ()))
VMEM_LIMIT = 48 * 1024 * 1024


def lane_iota(shape):
    return lax.broadcasted_iota(jnp.int32, shape, len(shape) - 1)


def gauss(coords, centres):
    offset = (coords - centres) * (2.0 / HALO * math.sqrt(LOG2E))
    return jnp.exp2(-(offset * offset))


def halves(value):
    high = value.astype(jnp.bfloat16)
    return high, (value - high.astype(jnp.float32)).astype(jnp.bfloat16)


def mix_halves(mix_ref, depth):
    high, low = halves(mix_ref[...])
    low = pltpu.roll(low.astype(jnp.float32), depth, 1)
    both = jnp.where(lane_iota(low.shape) < depth, high.astype(jnp.float32), low).astype(jnp.bfloat16)
    return jnp.concatenate([both, high[:, :depth]], 1)


def whole_blocks(live, size):
    return lax.div(live + (size - 1), size)


def in_batches(blocks, add):
    done = jnp.int32(0)
    for size in (MANY, MANY // 2, MANY // 4):
        spare = size // 2 - 1 if size > MANY // 4 else size - 1
        steps = lax.div(blocks - done + spare, size)

        def batch(c, carry, done=done, size=size):
            add(done + size * c, size)
            return carry

        lax.fori_loop(0, steps, batch, 0)
        done = jnp.minimum(done + size * steps, blocks)


def pick(table_row, index):
    return jnp.take_along_axis(jnp.broadcast_to(table_row, index.shape), index, axis=1, mode="promise_in_bounds")


def pack_columns(full):
    tail = full[24:32]
    lane = lane_iota((8, LANES))
    parts = []
    for part in range(3):
        moved = pltpu.roll(tail, 96 - 32 * part, 1)
        parts.append(jnp.where(lane < 96, full[8 * part : 8 * part + 8], moved))
    return jnp.concatenate(parts, 0)


def unpack_columns(dense):
    lane = lane_iota((8, LANES))
    first = pltpu.roll(dense[0:8], 32, 1)
    second = pltpu.roll(dense[8:16], 64, 1)
    third = pltpu.roll(dense[16:24], 96, 1)
    tail = jnp.where(lane < 32, first, jnp.where(lane < 64, second, third))
    return jnp.concatenate([dense, tail], 0)


def widen(ref_value):
    rows, cols = ref_value.shape
    return jnp.concatenate([ref_value, jnp.zeros((rows, LANES - cols), ref_value.dtype)], 1)


def column_tables(depth, levels, slabs, table_ref, up_ref, down_ref, mix_ref, inv_ref, square_ref):
    slab = lax.axis_index("gz")
    square_ref[...] = jnp.ones((LANES, LANES), jnp.float32)
    square_ref[0:CLASSES, 0:depth] = table_ref[...]
    square_ref[CLASSES : 2 * CLASSES, 0:depth] = THETA_SCALE * table_ref[...]
    inv_ref[...] = 1.0 / jnp.transpose(square_ref[...])[0:depth]
    value = jnp.ones((1, LANES), jnp.float32)
    flux = value
    high = value
    back = value
    up_ref[0:1, :] = value
    down_ref[depth - 1 : depth, :] = high
    for step in range(1, depth):
        value = value + flux * inv_ref[step : step + 1, :]
        flux = flux + value
        up_ref[step : step + 1, :] = value
        other = depth - 1 - step
        high = high + back * inv_ref[other + 1 : other + 2, :]
        back = back + high
        down_ref[other : other + 1, :] = high
    down_ref[...] = down_ref[...] * (1.0 / flux)
    level = lax.broadcasted_iota(jnp.int32, (depth, LANES), 0)
    lane = lane_iota((depth, LANES))
    below = jnp.where(level < slab * levels, up_ref[...], 0.0)
    above = jnp.where(level >= (slab + 1) * levels, down_ref[...], 0.0)
    mixed = jnp.where(lane < CLASSES, below, pltpu.roll(above, CLASSES, 1))
    square_ref[0:depth, :] = mixed
    square_ref[depth:LANES, :] = jnp.zeros((LANES - depth, LANES), jnp.float32)
    mix_ref[...] = jnp.transpose(square_ref[...])[0 : 2 * CLASSES, :]


def solve_field(in_ref, picks_ref, field, low, high, force_of, out_ref, gather_ref, copy_of):
    levels, _, cols = in_ref.shape
    for z in range(levels):
        right = force_of(z, widen(in_ref[z]))
        down = picks_ref[2 + field, z]
        low = low + picks_ref[field, z] * right
        gather_ref[0, z] = down * low
        gather_ref[1, z] = down * right
    for z in range(levels - 1, -1, -1):
        out_ref[z] = (gather_ref[0, z] + picks_ref[field, z] * high)[:, :cols]
        high = high + gather_ref[1, z]
        if copy_of is not None and z % (levels // PIECES) == 0:
            copy_of(z // (levels // PIECES)).start()


def own_kernel(slabs, u_hbm, theta_hbm, klass_hbm, table_ref, sent_ref,
               sums_ref, mix_ref, index_ref, acc_ref, u_ref, theta_ref, picks_ref,
               up_ref, down_ref, inv_ref, square_ref, klass_ref, gather_ref, sems):
    levels, rows, cols = u_ref.shape
    depth = levels * slabs
    slab = lax.axis_index("gz")
    part = levels // PIECES
    copies = [pltpu.make_async_copy(klass_hbm, klass_ref, sems.at[0])]
    for piece in range(PIECES):
        at = pl.ds(piece * part, part)
        copies.append(pltpu.make_async_copy(u_hbm.at[at], u_ref.at[at], sems.at[1 + 2 * piece]))
        copies.append(pltpu.make_async_copy(theta_hbm.at[at], theta_ref.at[at], sems.at[2 + 2 * piece]))
    for copy in copies:
        copy.start()
    live = jnp.max(sent_ref[32:40, :]).astype(jnp.int32)
    column_tables(depth, levels, slabs, table_ref, up_ref, down_ref, mix_ref, inv_ref, square_ref)
    acc_ref[...] = jnp.zeros_like(acc_ref)
    mix = mix_halves(mix_ref, depth)

    def add(first, n):
        entries = [(0, first + k, live, 0, 0) for k in range(n)]
        add_points(sent_ref, entries, mix, acc_ref, tuple(range(rows // FINE)), cols)

    in_batches(whole_blocks(live, LANES), add)
    copies[0].wait()
    index = widen(klass_ref[...])
    index_ref[...] = index
    zero = jnp.zeros(index.shape, jnp.float32)
    start = pl.multiple_of(slab * levels, levels)
    ups = up_ref[pl.ds(start, levels), :]
    downs = down_ref[pl.ds(start, levels), :]
    for z in range(levels):
        picks_ref[0, z] = pick(ups[z : z + 1], index)
        picks_ref[1, z] = pick(ups[z : z + 1], index + CLASSES)
        picks_ref[2, z] = pick(downs[z : z + 1], index)
        picks_ref[3, z] = pick(downs[z : z + 1], index + CLASSES)
    sums = [zero, zero, zero, zero]
    for copy in copies[1:]:
        copy.wait()
    for z in range(levels):
        u_rows = widen(u_ref[z])
        t_rows = widen(theta_ref[z])
        sums[0] = sums[0] + picks_ref[0, z] * u_rows
        sums[1] = sums[1] + picks_ref[1, z] * t_rows
        sums[2] = sums[2] + picks_ref[2, z] * u_rows
        sums[3] = sums[3] + picks_ref[3, z] * t_rows
    for number, part in enumerate(sums):
        sums_ref[24 * number : 24 * number + 24, :] = pack_columns(part)
    solve_field(theta_ref, picks_ref, 1, zero, zero, lambda z, right: right, theta_ref, gather_ref, None)


def pack_kernel(slabs, sums_ref, straight_ref, diagonal_ref, out_ref):
    slab = lax.axis_index("gz")
    counts = straight_ref[32:40, :] + pltpu.roll(diagonal_ref[32:40, :], LANES // 2, 1)
    for target in range(slabs):
        out_ref[target, 0:48, :] = jnp.where(target > slab, sums_ref[0:48, :], sums_ref[48:96, :])
        out_ref[target, 48:80, :] = straight_ref[0:32, :]
        out_ref[target, 80:112, :] = diagonal_ref[0:32, :]
        out_ref[target, 112:120, :] = counts


def heights(points_ref, entries, mix, levels):
    slab = lax.axis_index("gz")
    depth = mix.shape[1] // 3
    places = []
    parts = []
    for base, which, live, _, _ in entries:
        px, py, pz, weight = (points_ref[pl.ds(base + 8 * a + which, 1), :] for a in range(4))
        alive = which * LANES + lane_iota((1, LANES)) < live
        places.append((px, py, jnp.where(alive, weight, 0.0), alive))
        z = lax.broadcasted_iota(jnp.int32, (depth, LANES), 0)
        own = slab * levels + lax.broadcasted_iota(jnp.int32, (levels, LANES), 0)
        parts.append((gauss(z.astype(jnp.float32), pz), gauss(own.astype(jnp.float32), pz)))
    gz, own = (jnp.concatenate(both, 1) for both in zip(*parts))
    gz_high, gz_low = halves(gz)
    other = jnp.dot(mix, jnp.concatenate([gz_high, gz_high, gz_low], 0), preferred_element_type=jnp.float32)
    return places, jnp.concatenate([own, other], 0)


def left_halves(high, fine):
    deep, width = high.shape
    return halves((high[:, None, :] * fine[None]).reshape(deep * FINE, width))


def fine_and_coarse(place, steps):
    cell = lax.broadcasted_iota(jnp.int32, (FINE,) + place.shape[1:], 0).astype(jnp.float32)
    fine = gauss(cell, place)
    coarse = [jnp.exp2(LOG2E * (2.0 * step / FINE * place - float(step * step))) for step in steps]
    return fine, coarse


def add_points(points_ref, entries, mix, acc_ref, steps, cols):
    deep, rows, _ = acc_ref.shape
    tile_x, tile_y = (lax.axis_index(name) for name in ("gx", "gy"))
    places, high = heights(points_ref, entries, mix, deep - 2 * CLASSES)
    j = lax.broadcasted_iota(jnp.int32, (cols, LANES), 0).astype(jnp.float32)
    parts = []
    for px, py, weight, alive in places:
        x = jnp.where(alive, px - (tile_x * rows).astype(jnp.float32), 0.0)
        fine, coarse = fine_and_coarse(x, steps)
        gj = gauss(j, py - (tile_y * cols).astype(jnp.float32))
        parts.append([fine, gj] + [factor * weight for factor in coarse])
    fine, gj, *coarse = (jnp.concatenate(both, 1) for both in zip(*parts))
    gap = jnp.zeros((LANES - cols, gj.shape[1]), jnp.bfloat16)
    pairs = [halves(gj * factor) for factor in coarse]
    right_high = jnp.concatenate([x for pair in pairs for x in (pair[0], gap)], 0)
    right_low = jnp.concatenate([x for pair in pairs for x in (pair[1], gap)], 0)
    left_high, left_low = left_halves(high, fine)
    left = jnp.concatenate([left_high, left_low, left_high], 1)
    right = jnp.concatenate([right_high, right_high, right_low], 1)
    total = lax.dot_general(left, right, NT, preferred_element_type=jnp.float32)
    for number, step in enumerate(steps):
        part = total[:, number * LANES : (number + 1) * LANES].reshape(deep, FINE, LANES)
        acc_ref[:, step * FINE : (step + 1) * FINE, :] += part


def add_sides(points_ref, entries, mix, side_ref, rows, cols):
    deep = side_ref.shape[0]
    tile_x, tile_y = (lax.axis_index(name) for name in ("gx", "gy"))
    places, high = heights(points_ref, entries, mix, deep - 2 * CLASSES)
    i = lax.broadcasted_iota(jnp.int32, (rows, LANES), 0)
    parts = []
    for (px, py, weight, alive), (_, _, _, at_x, at_y) in zip(places, entries):
        before = at_y < tile_y
        y = py - (tile_y * cols).astype(jnp.float32)
        y = jnp.where(alive, jnp.where(before, y, float(cols - 1) - y), 0.0)
        fine, coarse = fine_and_coarse(y, (0, 1))
        backward = gauss(float(FINE - 1) - lax.broadcasted_iota(jnp.int32, fine.shape, 0).astype(jnp.float32), y)
        inner = i - ((at_x - tile_x) * rows - HALO)
        gi = gauss(i.astype(jnp.float32), px - (tile_x * rows).astype(jnp.float32)) * weight
        gi = jnp.where((inner >= 0) & (inner < rows + 2 * HALO), gi, 0.0)
        gi = jnp.concatenate([jnp.where(before, gi, 0.0), jnp.where(before, 0.0, gi)], 0)
        parts.append((jnp.where(before, fine, backward), gi, coarse[0], coarse[1]))
    fine, gi, *coarse = (jnp.concatenate(both, 1) for both in zip(*parts))
    right_high, right_low = halves(jnp.concatenate([gi * factor for factor in coarse], 0))
    right = jnp.concatenate(
        [jnp.concatenate([right_high, right_low], 0), jnp.concatenate([right_high, jnp.zeros_like(right_low)], 0)], 1
    )
    left = jnp.concatenate(left_halves(high, fine), 1)
    total = lax.dot_general(left, right, NT, preferred_element_type=jnp.float32)
    side_ref[...] += (total[:, :LANES] + total[:, LANES:]).reshape(side_ref.shape)


def cross_factor(step, cell):
    return jnp.exp2((-2.0 * LOG2E / FINE) * (step * cell).astype(jnp.float32))


def by_class(value_of, index):
    low = jnp.zeros(index.shape, jnp.float32)
    high = low
    for c in range(CLASSES):
        here = index == c
        low = jnp.where(here, value_of(c), low)
        high = jnp.where(here, value_of(CLASSES + c), high)
    return low, high


def side_fields(side_ref, index_ref, stack_ref, rows, cols):
    levels = side_ref.shape[0] - 2 * CLASSES
    square = jnp.concatenate([index_ref[...], jnp.zeros((LANES - rows, LANES), jnp.int32)], 0)
    square = jnp.transpose(square.astype(jnp.float32))
    first = square[0:HALO]
    last = pltpu.roll(square[cols - HALO : cols], rows, 1)
    index = jnp.where(lane_iota(first.shape) < rows, first, last).astype(jnp.int32)

    lane = lane_iota((FINE, LANES))
    line = lax.broadcasted_iota(jnp.int32, (FINE, LANES), 0)
    on_first = lane % (2 * rows) < rows
    cross = cross_factor(lane // (2 * rows), jnp.where(on_first, line, FINE - 1 - line))

    def folded(z):
        near = side_ref[z] * cross
        far = pltpu.roll(near, 2 * rows, 1)
        return jnp.concatenate([jnp.where(lane < rows, near, far), jnp.where(lane < rows, far, near)], 0)

    for z in range(levels):
        stack_ref[z * HALO : (z + 1) * HALO, :] = folded(z)
    low, high = by_class(lambda c: folded(levels + c), index)
    stack_ref[levels * HALO : (levels + 1) * HALO, :] = low
    stack_ref[(levels + 1) * HALO : (levels + 2) * HALO, :] = high
    wide = lane_iota((rows, LANES))
    fields = []
    per = LANES // HALO
    for group in range(stack_ref.shape[0] // LANES):
        turned = jnp.transpose(stack_ref[group * LANES : (group + 1) * LANES, :])
        for k in range(per):
            if group * per + k < levels + 2:
                before = pltpu.roll(turned[0:rows], (LANES - k * HALO) % LANES, 1)
                after = pltpu.roll(turned[rows : 2 * rows], (LANES + cols - HALO - k * HALO) % LANES, 1)
                fields.append(jnp.where(wide < HALO, before, jnp.where((wide >= cols - HALO) & (wide < cols), after, 0.0)))
    return fields


def last_kernel(slabs, got_ref, own_ref, u_ref, theta_ref, index_ref, picks_ref, mix_ref, u_out, theta_out,
                acc_ref, points_ref, side_ref, stack_ref, gather_ref, u_new, theta_new,
                live_ref, at_ref, list_ref, out_sems):
    levels, rows, cols = u_ref.shape

    def out_copy(field, piece):
        source, target = ((u_new, u_out), (theta_new, theta_out))[field]
        part = pl.ds(piece * (levels // PIECES), levels // PIECES)
        return pltpu.make_async_copy(source.at[part], target.at[part], out_sems.at[field, piece])

    tile_x, tile_y, slab = (lax.axis_index(name) for name in ("gx", "gy", "gz"))
    depth = levels * slabs
    mix = mix_halves(mix_ref, depth)
    lane8 = lane_iota((8, LANES))
    low_sum = jnp.zeros((48, LANES), jnp.float32)
    high_sum = low_sum
    for source in range(slabs):
        points_ref[source * 32 : source * 32 + 32, :] = got_ref[source, 48:80, :]
        points_ref[(source + slabs) * 32 : (source + slabs) * 32 + 32, :] = got_ref[source, 80:112, :]
        counts = got_ref[source, 112:120, :]
        live_ref[source] = jnp.max(jnp.where(lane8 < LANES // 2, counts, 0.0)).astype(jnp.int32)
        live_ref[source + slabs] = jnp.max(jnp.where(lane8 < LANES // 2, 0.0, counts)).astype(jnp.int32)
        edge = got_ref[source, 0:48, :]
        low_sum = low_sum + jnp.where(source < slab, edge, 0.0)
        high_sum = high_sum + jnp.where(source > slab, edge, 0.0)
    points_ref[SPARE * 32 : SPARE * 32 + 32, :] = jnp.zeros((32, LANES), jnp.float32)
    live_ref[SPARE] = 0
    for number, (dx, dy) in enumerate(TILES + ((0, 1),)):
        at_ref[2 * number] = tile_x + dx
        at_ref[2 * number + 1] = tile_y + dy

    index = index_ref[...]
    low = unpack_columns(low_sum[24:48])[:, :cols]
    high = unpack_columns(high_sum[24:48])[:, :cols]
    for z in range(levels):
        other = picks_ref[3, z][:, :cols] * low + picks_ref[1, z][:, :cols] * high
        theta_new[z] = theta_ref[z] + other
        if (z + 1) % (levels // PIECES) == 0:
            out_copy(1, z // (levels // PIECES)).start()

    acc_ref[...] = own_ref[...]
    for number, steps in ((0, (0, 1)), (1, (rows // FINE - 2, rows // FINE - 1))):
        live = live_ref[number]

        def add(first, n):
            entries = [(number * 32, first + k, live, 0, 0) for k in range(n)]
            add_points(points_ref, entries, mix, acc_ref, steps, cols)

        in_batches(whole_blocks(live, LANES), add)

    filled = jnp.int32(0)
    for number in ACROSS:
        for k in range(8):
            list_ref[filled + k] = number * 8 + k
        filled = filled + whole_blocks(live_ref[number], LANES)
    for k in range(MANY):
        list_ref[filled + k] = SPARE * 8
    side_ref[...] = jnp.zeros_like(side_ref)
    stack_ref[...] = jnp.zeros_like(stack_ref)

    def add_side(first, n):
        entries = []
        for k in range(n):
            entry = list_ref[first + k]
            number = lax.shift_right_logical(entry, 3)
            entries.append((number * 32, lax.bitwise_and(entry, 7), live_ref[number], at_ref[2 * number],
                            at_ref[2 * number + 1]))
        add_sides(points_ref, entries, mix, side_ref, rows, cols)

    in_batches(filled, add_side)
    fields = side_fields(side_ref, index_ref, stack_ref, rows, cols)
    row = lax.broadcasted_iota(jnp.int32, (rows, LANES), 0)
    cross = cross_factor(row // FINE, row % FINE)
    low_force, high_force = by_class(lambda c: acc_ref[levels + c], index)
    solve_field(u_ref, picks_ref, 0,
                unpack_columns(low_sum[0:24]) + low_force * cross + fields[levels],
                unpack_columns(high_sum[0:24]) + high_force * cross + fields[levels + 1],
                lambda z, right: right + acc_ref[z] * cross + fields[z], u_new, gather_ref, functools.partial(out_copy, 0))
    for field in range(2):
        for piece in range(PIECES):
            out_copy(field, piece).wait()


def lateral(offsets, tiles_x, tiles_y, slabs):
    pairs = []
    for x in range(tiles_x):
        for y in range(tiles_y):
            for t in range(slabs):
                sx, sy = x + offsets[t][0], y + offsets[t][1]
                if 0 <= sx < tiles_x and 0 <= sy < tiles_y:
                    pairs.append(((sx * tiles_y + sy) * slabs + t, (x * tiles_y + y) * slabs + t))
    return pairs


def shards(u_wind, theta, act_points, point_count, klass, diff_table):
    levels, rows, cols = u_wind.shape
    tiles_x, tiles_y, slabs = (lax.axis_size(name) for name in ("gx", "gy", "gz"))
    depth = levels * slabs
    f32 = jnp.float32
    stay = lambda x: pltpu.with_memory_space_constraint(x, pltpu.HBM)
    u_wind, theta, klass = stay(u_wind), stay(theta), stay(klass)
    vmem = pl.BlockSpec(memory_space=pltpu.VMEM)
    hbm = pl.BlockSpec(memory_space=pltpu.HBM)
    params = pltpu.CompilerParams(vmem_limit_bytes=VMEM_LIMIT)
    sent = jnp.pad(act_points.reshape(32, LANES), ((0, 8), (0, 0)))
    sent = lax.dynamic_update_slice(sent, point_count.astype(f32), (32 + lax.axis_index("gz"), 0))
    axes = ("gx", "gy", "gz")
    straight = lax.ppermute(sent, axes, lateral(STRAIGHT, tiles_x, tiles_y, slabs))
    diagonal = lax.ppermute(sent, axes, lateral(DIAGONAL, tiles_x, tiles_y, slabs))
    acc_shape = (levels + 2 * CLASSES, rows, LANES)
    field = pltpu.VMEM(u_wind.shape, f32)
    sums, mix, index, own, u_here, theta_here, picks = pl.pallas_call(
        functools.partial(own_kernel, slabs),
        out_shape=[
            jax.ShapeDtypeStruct((96, LANES), f32),
            jax.ShapeDtypeStruct((2 * CLASSES, LANES), f32),
            jax.ShapeDtypeStruct((rows, LANES), jnp.int32),
            jax.ShapeDtypeStruct(acc_shape, f32),
            jax.ShapeDtypeStruct(u_wind.shape, f32),
            jax.ShapeDtypeStruct(u_wind.shape, f32),
            jax.ShapeDtypeStruct((4, levels, rows, LANES), f32),
        ],
        in_specs=[hbm, hbm, hbm, vmem, vmem],
        out_specs=[vmem] * 7,
        scratch_shapes=[
            pltpu.VMEM((depth, LANES), f32),
            pltpu.VMEM((depth, LANES), f32),
            pltpu.VMEM((depth, LANES), f32),
            pltpu.VMEM((LANES, LANES), f32),
            pltpu.VMEM((rows, cols), jnp.int32),
            pltpu.VMEM((2, levels, rows, LANES), f32),
            pltpu.SemaphoreType.DMA((1 + 2 * PIECES,)),
        ],
        compiler_params=params,
        cost_estimate=pl.CostEstimate(flops=2 * 10**9, bytes_accessed=10**6, transcendentals=10**5),
        name="own_tile",
    )(u_wind, theta, klass, diff_table, sent)
    packed = pl.pallas_call(
        functools.partial(pack_kernel, slabs),
        out_shape=jax.ShapeDtypeStruct((slabs, 120, LANES), f32),
        compiler_params=params,
        name="pack",
    )(sums, straight, diagonal)
    got = lax.all_to_all(packed, "gz", 0, 0)
    return pl.pallas_call(
        functools.partial(last_kernel, slabs),
        out_shape=[jax.ShapeDtypeStruct(u_wind.shape, f32)] * 2,
        in_specs=[vmem] * 7,
        out_specs=[hbm] * 2,
        scratch_shapes=[
            pltpu.VMEM(acc_shape, f32),
            pltpu.VMEM(((SPARE + 1) * 32, LANES), f32),
            pltpu.VMEM((levels + 2 * CLASSES, FINE, LANES), f32),
            pltpu.VMEM((3 * LANES, LANES), f32),
            pltpu.VMEM((2, levels, rows, LANES), f32),
            field,
            field,
            pltpu.SMEM((SPARE + 1,), jnp.int32),
            pltpu.SMEM((2 * SPARE + 2,), jnp.int32),
            pltpu.SMEM((8 * SPARE,), jnp.int32),
            pltpu.SemaphoreType.DMA((2, PIECES)),
        ],
        compiler_params=params,
        name="solve",
    )(got, own, u_here, theta_here, index, picks, mix)


def solution(mesh):
    return jax.shard_map(
        shards,
        mesh=mesh,
        in_specs=(
            P("gz", "gx", "gy"),
            P("gz", "gx", "gy"),
            P(None, "gx", "gy", None),
            P("gx", "gy"),
            P("gx", "gy"),
            P(),
        ),
        out_specs=(P("gz", "gx", "gy"), P("gz", "gx", "gy")),
        check_vma=False,
    )
```

```python
import functools
import math

import jax
import jax.numpy as jnp
from jax import lax
from jax.experimental import pallas as pl
from jax.experimental.pallas import tpu as pltpu
from jax.sharding import PartitionSpec as P

HALO = 16
THETA_SCALE = 1.25
CLASSES = 16
LANES = 128
STRAIGHT = ((-1, 0), (1, 0), (0, -1), (0, 1))
DIAGONAL = ((-1, -1), (1, 1), (1, -1), (-1, 1))
TILES = STRAIGHT + DIAGONAL
SPARE = len(TILES)
PIECES = 4
FINE = HALO // 2
LOG2E = math.log2(math.e)
ACROSS = (2, 3, 4, 5, 6, 7)
NT = (((1,), (1,)), ((), ()))
VMEM_LIMIT = 48 * 1024 * 1024


def lane_iota(shape):
    return lax.broadcasted_iota(jnp.int32, shape, len(shape) - 1)


def gauss(coords, centres):
    offset = (coords - centres) * (2.0 / HALO * math.sqrt(LOG2E))
    return jnp.exp2(-(offset * offset))


def halves(value):
    high = value.astype(jnp.bfloat16)
    return high, (value - high.astype(jnp.float32)).astype(jnp.bfloat16)


def mix_halves(mix_ref, depth):
    high, low = halves(mix_ref[...])
    low = pltpu.roll(low.astype(jnp.float32), depth, 1)
    both = jnp.where(lane_iota(low.shape) < depth, high.astype(jnp.float32), low).astype(jnp.bfloat16)
    return jnp.concatenate([both, high[:, :depth]], 1)


def whole_blocks(live, size):
    return lax.div(live + (size - 1), size)


def in_batches(blocks, add, sizes):
    done = jnp.int32(0)
    for size in sizes:
        spare = size // 2 - 1 if size > sizes[-1] else size - 1
        steps = lax.div(blocks - done + spare, size)

        def batch(c, carry, done=done, size=size):
            add(done + size * c, size)
            return carry

        lax.fori_loop(0, steps, batch, 0)
        done = jnp.minimum(done + size * steps, blocks)


def pick(table_row, index):
    return jnp.take_along_axis(jnp.broadcast_to(table_row, index.shape), index, axis=1, mode="promise_in_bounds")


def pack_columns(full):
    tail = full[24:32]
    lane = lane_iota((8, LANES))
    parts = []
    for part in range(3):
        moved = pltpu.roll(tail, 96 - 32 * part, 1)
        parts.append(jnp.where(lane < 96, full[8 * part : 8 * part + 8], moved))
    return jnp.concatenate(parts, 0)


def unpack_columns(dense):
    lane = lane_iota((8, LANES))
    first = pltpu.roll(dense[0:8], 32, 1)
    second = pltpu.roll(dense[8:16], 64, 1)
    third = pltpu.roll(dense[16:24], 96, 1)
    tail = jnp.where(lane < 32, first, jnp.where(lane < 64, second, third))
    return jnp.concatenate([dense, tail], 0)


def widen(ref_value):
    rows, cols = ref_value.shape
    return jnp.concatenate([ref_value, jnp.zeros((rows, LANES - cols), ref_value.dtype)], 1)


def column_tables(depth, levels, slabs, table_ref, up_ref, down_ref, mix_ref, inv_ref, square_ref):
    slab = lax.axis_index("gz")
    square_ref[...] = jnp.ones((LANES, LANES), jnp.float32)
    square_ref[0:CLASSES, 0:depth] = table_ref[...]
    square_ref[CLASSES : 2 * CLASSES, 0:depth] = THETA_SCALE * table_ref[...]
    inv_ref[...] = 1.0 / jnp.transpose(square_ref[...])[0:depth]
    value = jnp.ones((1, LANES), jnp.float32)
    flux = value
    high = value
    back = value
    up_ref[0:1, :] = value
    down_ref[depth - 1 : depth, :] = high
    for step in range(1, depth):
        value = value + flux * inv_ref[step : step + 1, :]
        flux = flux + value
        up_ref[step : step + 1, :] = value
        other = depth - 1 - step
        high = high + back * inv_ref[other + 1 : other + 2, :]
        back = back + high
        down_ref[other : other + 1, :] = high
    down_ref[...] = down_ref[...] * (1.0 / flux)
    level = lax.broadcasted_iota(jnp.int32, (depth, LANES), 0)
    lane = lane_iota((depth, LANES))
    below = jnp.where(level < slab * levels, up_ref[...], 0.0)
    above = jnp.where(level >= (slab + 1) * levels, down_ref[...], 0.0)
    mixed = jnp.where(lane < CLASSES, below, pltpu.roll(above, CLASSES, 1))
    square_ref[0:depth, :] = mixed
    square_ref[depth:LANES, :] = jnp.zeros((LANES - depth, LANES), jnp.float32)
    mix_ref[...] = jnp.transpose(square_ref[...])[0 : 2 * CLASSES, :]


def solve_field(in_ref, picks_ref, field, low, high, force_of, out_ref, gather_ref, copy_of):
    levels, _, cols = in_ref.shape
    for z in range(levels):
        right = force_of(z, widen(in_ref[z]))
        down = picks_ref[2 + field, z]
        low = low + picks_ref[field, z] * right
        gather_ref[0, z] = down * low
        gather_ref[1, z] = down * right
    for z in range(levels - 1, -1, -1):
        out_ref[z] = (gather_ref[0, z] + picks_ref[field, z] * high)[:, :cols]
        high = high + gather_ref[1, z]
        if copy_of is not None and z % (levels // PIECES) == 0:
            copy_of(z // (levels // PIECES)).start()


def own_kernel(slabs, u_hbm, theta_hbm, klass_hbm, table_ref, sent_ref,
               sums_ref, mix_ref, index_ref, acc_ref, u_ref, theta_ref, picks_ref,
               up_ref, down_ref, inv_ref, square_ref, klass_ref, gather_ref, sems):
    levels, rows, cols = u_ref.shape
    depth = levels * slabs
    slab = lax.axis_index("gz")
    part = levels // PIECES
    copies = [pltpu.make_async_copy(klass_hbm, klass_ref, sems.at[0])]
    for piece in range(PIECES):
        at = pl.ds(piece * part, part)
        copies.append(pltpu.make_async_copy(u_hbm.at[at], u_ref.at[at], sems.at[1 + 2 * piece]))
        copies.append(pltpu.make_async_copy(theta_hbm.at[at], theta_ref.at[at], sems.at[2 + 2 * piece]))
    for copy in copies:
        copy.start()
    live = jnp.max(sent_ref[32:40, :]).astype(jnp.int32)
    column_tables(depth, levels, slabs, table_ref, up_ref, down_ref, mix_ref, inv_ref, square_ref)
    acc_ref[...] = jnp.zeros_like(acc_ref)
    mix = mix_halves(mix_ref, depth)

    def add(first, n):
        entries = [(0, first + k, live, 0, 0) for k in range(n)]
        add_points(sent_ref, entries, mix, acc_ref, tuple(range(rows // FINE)), cols)

    in_batches(whole_blocks(live, LANES), add, (8, 4, 2))
    copies[0].wait()
    index = widen(klass_ref[...])
    index_ref[...] = index
    zero = jnp.zeros(index.shape, jnp.float32)
    start = pl.multiple_of(slab * levels, levels)
    ups = up_ref[pl.ds(start, levels), :]
    downs = down_ref[pl.ds(start, levels), :]
    for z in range(levels):
        picks_ref[0, z] = pick(ups[z : z + 1], index)
        picks_ref[1, z] = pick(ups[z : z + 1], index + CLASSES)
        picks_ref[2, z] = pick(downs[z : z + 1], index)
        picks_ref[3, z] = pick(downs[z : z + 1], index + CLASSES)
    sums = [zero, zero, zero, zero]
    for copy in copies[1:]:
        copy.wait()
    for z in range(levels):
        u_rows = widen(u_ref[z])
        t_rows = widen(theta_ref[z])
        sums[0] = sums[0] + picks_ref[0, z] * u_rows
        sums[1] = sums[1] + picks_ref[1, z] * t_rows
        sums[2] = sums[2] + picks_ref[2, z] * u_rows
        sums[3] = sums[3] + picks_ref[3, z] * t_rows
    for number, part in enumerate(sums):
        sums_ref[24 * number : 24 * number + 24, :] = pack_columns(part)
    solve_field(theta_ref, picks_ref, 1, zero, zero, lambda z, right: right, theta_ref, gather_ref, None)


def pack_kernel(slabs, sums_ref, straight_ref, diagonal_ref, out_ref):
    slab = lax.axis_index("gz")
    counts = straight_ref[32:40, :] + pltpu.roll(diagonal_ref[32:40, :], LANES // 2, 1)
    for target in range(slabs):
        out_ref[target, 0:48, :] = jnp.where(target > slab, sums_ref[0:48, :], sums_ref[48:96, :])
        out_ref[target, 48:80, :] = straight_ref[0:32, :]
        out_ref[target, 80:112, :] = diagonal_ref[0:32, :]
        out_ref[target, 112:120, :] = counts


def heights(points_ref, entries, mix, levels):
    slab = lax.axis_index("gz")
    depth = mix.shape[1] // 3
    places = []
    parts = []
    for base, which, live, _, _ in entries:
        px, py, pz, weight = (points_ref[pl.ds(base + 8 * a + which, 1), :] for a in range(4))
        alive = which * LANES + lane_iota((1, LANES)) < live
        places.append((px, py, jnp.where(alive, weight, 0.0), alive))
        z = lax.broadcasted_iota(jnp.int32, (depth, LANES), 0)
        own = slab * levels + lax.broadcasted_iota(jnp.int32, (levels, LANES), 0)
        parts.append((gauss(z.astype(jnp.float32), pz), gauss(own.astype(jnp.float32), pz)))
    gz, own = (jnp.concatenate(both, 1) for both in zip(*parts))
    gz_high, gz_low = halves(gz)
    other = jnp.dot(mix, jnp.concatenate([gz_high, gz_high, gz_low], 0), preferred_element_type=jnp.float32)
    return places, jnp.concatenate([own, other], 0)


def left_halves(high, fine):
    deep, width = high.shape
    return halves((high[:, None, :] * fine[None]).reshape(deep * FINE, width))


def fine_and_coarse(place, steps):
    cell = lax.broadcasted_iota(jnp.int32, (FINE,) + place.shape[1:], 0).astype(jnp.float32)
    fine = gauss(cell, place)
    coarse = [jnp.exp2(LOG2E * (2.0 * step / FINE * place - float(step * step))) for step in steps]
    return fine, coarse


def add_points(points_ref, entries, mix, acc_ref, steps, cols):
    deep, rows, _ = acc_ref.shape
    tile_x, tile_y = (lax.axis_index(name) for name in ("gx", "gy"))
    places, high = heights(points_ref, entries, mix, deep - 2 * CLASSES)
    j = lax.broadcasted_iota(jnp.int32, (cols, LANES), 0).astype(jnp.float32)
    parts = []
    for px, py, weight, alive in places:
        x = jnp.where(alive, px - (tile_x * rows).astype(jnp.float32), 0.0)
        fine, coarse = fine_and_coarse(x, steps)
        gj = gauss(j, py - (tile_y * cols).astype(jnp.float32))
        parts.append([fine, gj] + [factor * weight for factor in coarse])
    fine, gj, *coarse = (jnp.concatenate(both, 1) for both in zip(*parts))
    gap = jnp.zeros((LANES - cols, gj.shape[1]), jnp.bfloat16)
    pairs = [halves(gj * factor) for factor in coarse]
    right_high = jnp.concatenate([x for pair in pairs for x in (pair[0], gap)], 0)
    right_low = jnp.concatenate([x for pair in pairs for x in (pair[1], gap)], 0)
    left_high, left_low = left_halves(high, fine)
    left = jnp.concatenate([left_high, left_low, left_high], 1)
    right = jnp.concatenate([right_high, right_high, right_low], 1)
    total = lax.dot_general(left, right, NT, preferred_element_type=jnp.float32)
    for number, step in enumerate(steps):
        part = total[:, number * LANES : (number + 1) * LANES].reshape(deep, FINE, LANES)
        acc_ref[:, step * FINE : (step + 1) * FINE, :] += part


def add_sides(points_ref, entries, mix, side_ref, rows, cols):
    deep = side_ref.shape[0]
    tile_x, tile_y = (lax.axis_index(name) for name in ("gx", "gy"))
    places, high = heights(points_ref, entries, mix, deep - 2 * CLASSES)
    i = lax.broadcasted_iota(jnp.int32, (rows, LANES), 0)
    parts = []
    for (px, py, weight, alive), (_, _, _, at_x, at_y) in zip(places, entries):
        before = at_y < tile_y
        y = py - (tile_y * cols).astype(jnp.float32)
        y = jnp.where(alive, jnp.where(before, y, float(cols - 1) - y), 0.0)
        fine, coarse = fine_and_coarse(y, (0, 1))
        backward = gauss(float(FINE - 1) - lax.broadcasted_iota(jnp.int32, fine.shape, 0).astype(jnp.float32), y)
        inner = i - ((at_x - tile_x) * rows - HALO)
        gi = gauss(i.astype(jnp.float32), px - (tile_x * rows).astype(jnp.float32)) * weight
        gi = jnp.where((inner >= 0) & (inner < rows + 2 * HALO), gi, 0.0)
        gi = jnp.concatenate([jnp.where(before, gi, 0.0), jnp.where(before, 0.0, gi)], 0)
        parts.append((jnp.where(before, fine, backward), gi, coarse[0], coarse[1]))
    fine, gi, *coarse = (jnp.concatenate(both, 1) for both in zip(*parts))
    right_high, right_low = halves(jnp.concatenate([gi * factor for factor in coarse], 0))
    right = jnp.concatenate(
        [jnp.concatenate([right_high, right_low], 0), jnp.concatenate([right_high, jnp.zeros_like(right_low)], 0)], 1
    )
    left = jnp.concatenate(left_halves(high, fine), 1)
    total = lax.dot_general(left, right, NT, preferred_element_type=jnp.float32)
    side_ref[...] += (total[:, :LANES] + total[:, LANES:]).reshape(side_ref.shape)


def cross_factor(step, cell):
    return jnp.exp2((-2.0 * LOG2E / FINE) * (step * cell).astype(jnp.float32))


def by_class(value_of, index):
    low = jnp.zeros(index.shape, jnp.float32)
    high = low
    for c in range(CLASSES):
        here = index == c
        low = jnp.where(here, value_of(c), low)
        high = jnp.where(here, value_of(CLASSES + c), high)
    return low, high


def side_fields(side_ref, index_ref, stack_ref, rows, cols):
    levels = side_ref.shape[0] - 2 * CLASSES
    square = jnp.concatenate([index_ref[...], jnp.zeros((LANES - rows, LANES), jnp.int32)], 0)
    square = jnp.transpose(square.astype(jnp.float32))
    first = square[0:HALO]
    last = pltpu.roll(square[cols - HALO : cols], rows, 1)
    index = jnp.where(lane_iota(first.shape) < rows, first, last).astype(jnp.int32)

    lane = lane_iota((FINE, LANES))
    line = lax.broadcasted_iota(jnp.int32, (FINE, LANES), 0)
    on_first = lane % (2 * rows) < rows
    cross = cross_factor(lane // (2 * rows), jnp.where(on_first, line, FINE - 1 - line))

    def folded(z):
        near = side_ref[z] * cross
        far = pltpu.roll(near, 2 * rows, 1)
        return jnp.concatenate([jnp.where(lane < rows, near, far), jnp.where(lane < rows, far, near)], 0)

    for z in range(levels):
        stack_ref[z * HALO : (z + 1) * HALO, :] = folded(z)
    low, high = by_class(lambda c: folded(levels + c), index)
    stack_ref[levels * HALO : (levels + 1) * HALO, :] = low
    stack_ref[(levels + 1) * HALO : (levels + 2) * HALO, :] = high
    wide = lane_iota((rows, LANES))
    fields = []
    per = LANES // HALO
    for group in range(stack_ref.shape[0] // LANES):
        turned = jnp.transpose(stack_ref[group * LANES : (group + 1) * LANES, :])
        for k in range(per):
            if group * per + k < levels + 2:
                before = pltpu.roll(turned[0:rows], (LANES - k * HALO) % LANES, 1)
                after = pltpu.roll(turned[rows : 2 * rows], (LANES + cols - HALO - k * HALO) % LANES, 1)
                fields.append(jnp.where(wide < HALO, before, jnp.where((wide >= cols - HALO) & (wide < cols), after, 0.0)))
    return fields


def last_kernel(slabs, got_ref, own_ref, u_ref, theta_ref, index_ref, picks_ref, mix_ref, u_out, theta_out,
                acc_ref, points_ref, side_ref, stack_ref, gather_ref, u_new, theta_new,
                live_ref, at_ref, list_ref, out_sems):
    levels, rows, cols = u_ref.shape

    def out_copy(field, piece):
        source, target = ((u_new, u_out), (theta_new, theta_out))[field]
        part = pl.ds(piece * (levels // PIECES), levels // PIECES)
        return pltpu.make_async_copy(source.at[part], target.at[part], out_sems.at[field, piece])

    tile_x, tile_y, slab = (lax.axis_index(name) for name in ("gx", "gy", "gz"))
    depth = levels * slabs
    mix = mix_halves(mix_ref, depth)
    lane8 = lane_iota((8, LANES))
    low_sum = jnp.zeros((48, LANES), jnp.float32)
    high_sum = low_sum
    for source in range(slabs):
        points_ref[source * 32 : source * 32 + 32, :] = got_ref[source, 48:80, :]
        points_ref[(source + slabs) * 32 : (source + slabs) * 32 + 32, :] = got_ref[source, 80:112, :]
        counts = got_ref[source, 112:120, :]
        live_ref[source] = jnp.max(jnp.where(lane8 < LANES // 2, counts, 0.0)).astype(jnp.int32)
        live_ref[source + slabs] = jnp.max(jnp.where(lane8 < LANES // 2, 0.0, counts)).astype(jnp.int32)
        edge = got_ref[source, 0:48, :]
        low_sum = low_sum + jnp.where(source < slab, edge, 0.0)
        high_sum = high_sum + jnp.where(source > slab, edge, 0.0)
    points_ref[SPARE * 32 : SPARE * 32 + 32, :] = jnp.zeros((32, LANES), jnp.float32)
    live_ref[SPARE] = 0
    for number, (dx, dy) in enumerate(TILES + ((0, 1),)):
        at_ref[2 * number] = tile_x + dx
        at_ref[2 * number + 1] = tile_y + dy

    index = index_ref[...]
    low = unpack_columns(low_sum[24:48])[:, :cols]
    high = unpack_columns(high_sum[24:48])[:, :cols]
    for z in range(levels):
        other = picks_ref[3, z][:, :cols] * low + picks_ref[1, z][:, :cols] * high
        theta_new[z] = theta_ref[z] + other
        if (z + 1) % (levels // PIECES) == 0:
            out_copy(1, z // (levels // PIECES)).start()

    acc_ref[...] = own_ref[...]
    for number, steps in ((0, (0, 1)), (1, (rows // FINE - 2, rows // FINE - 1))):
        live = live_ref[number]

        def add(first, n):
            entries = [(number * 32, first + k, live, 0, 0) for k in range(n)]
            add_points(points_ref, entries, mix, acc_ref, steps, cols)

        in_batches(whole_blocks(live, LANES), add, (8, 4, 2))

    filled = jnp.int32(0)
    for number in ACROSS:
        for k in range(8):
            list_ref[filled + k] = number * 8 + k
        filled = filled + whole_blocks(live_ref[number], LANES)
    for k in range(8):
        list_ref[filled + k] = SPARE * 8
    side_ref[...] = jnp.zeros_like(side_ref)
    stack_ref[...] = jnp.zeros_like(stack_ref)

    def add_side(first, n):
        entries = []
        for k in range(n):
            entry = list_ref[first + k]
            number = lax.shift_right_logical(entry, 3)
            entries.append((number * 32, lax.bitwise_and(entry, 7), live_ref[number], at_ref[2 * number],
                            at_ref[2 * number + 1]))
        add_sides(points_ref, entries, mix, side_ref, rows, cols)

    in_batches(filled, add_side, (16, 8, 4, 2))
    fields = side_fields(side_ref, index_ref, stack_ref, rows, cols)
    row = lax.broadcasted_iota(jnp.int32, (rows, LANES), 0)
    cross = cross_factor(row // FINE, row % FINE)
    low_force, high_force = by_class(lambda c: acc_ref[levels + c], index)
    solve_field(u_ref, picks_ref, 0,
                unpack_columns(low_sum[0:24]) + low_force * cross + fields[levels],
                unpack_columns(high_sum[0:24]) + high_force * cross + fields[levels + 1],
                lambda z, right: right + acc_ref[z] * cross + fields[z], u_new, gather_ref, functools.partial(out_copy, 0))
    for field in range(2):
        for piece in range(PIECES):
            out_copy(field, piece).wait()


def lateral(offsets, tiles_x, tiles_y, slabs):
    pairs = []
    for x in range(tiles_x):
        for y in range(tiles_y):
            for t in range(slabs):
                sx, sy = x + offsets[t][0], y + offsets[t][1]
                if 0 <= sx < tiles_x and 0 <= sy < tiles_y:
                    pairs.append(((sx * tiles_y + sy) * slabs + t, (x * tiles_y + y) * slabs + t))
    return pairs


def shards(u_wind, theta, act_points, point_count, klass, diff_table):
    levels, rows, cols = u_wind.shape
    tiles_x, tiles_y, slabs = (lax.axis_size(name) for name in ("gx", "gy", "gz"))
    depth = levels * slabs
    f32 = jnp.float32
    stay = lambda x: pltpu.with_memory_space_constraint(x, pltpu.HBM)
    u_wind, theta, klass = stay(u_wind), stay(theta), stay(klass)
    vmem = pl.BlockSpec(memory_space=pltpu.VMEM)
    hbm = pl.BlockSpec(memory_space=pltpu.HBM)
    params = pltpu.CompilerParams(vmem_limit_bytes=VMEM_LIMIT)
    sent = jnp.pad(act_points.reshape(32, LANES), ((0, 8), (0, 0)))
    sent = lax.dynamic_update_slice(sent, point_count.astype(f32), (32 + lax.axis_index("gz"), 0))
    axes = ("gx", "gy", "gz")
    straight = lax.ppermute(sent, axes, lateral(STRAIGHT, tiles_x, tiles_y, slabs))
    diagonal = lax.ppermute(sent, axes, lateral(DIAGONAL, tiles_x, tiles_y, slabs))
    acc_shape = (levels + 2 * CLASSES, rows, LANES)
    field = pltpu.VMEM(u_wind.shape, f32)
    sums, mix, index, own, u_here, theta_here, picks = pl.pallas_call(
        functools.partial(own_kernel, slabs),
        out_shape=[
            jax.ShapeDtypeStruct((96, LANES), f32),
            jax.ShapeDtypeStruct((2 * CLASSES, LANES), f32),
            jax.ShapeDtypeStruct((rows, LANES), jnp.int32),
            jax.ShapeDtypeStruct(acc_shape, f32),
            jax.ShapeDtypeStruct(u_wind.shape, f32),
            jax.ShapeDtypeStruct(u_wind.shape, f32),
            jax.ShapeDtypeStruct((4, levels, rows, LANES), f32),
        ],
        in_specs=[hbm, hbm, hbm, vmem, vmem],
        out_specs=[vmem] * 7,
        scratch_shapes=[
            pltpu.VMEM((depth, LANES), f32),
            pltpu.VMEM((depth, LANES), f32),
            pltpu.VMEM((depth, LANES), f32),
            pltpu.VMEM((LANES, LANES), f32),
            pltpu.VMEM((rows, cols), jnp.int32),
            pltpu.VMEM((2, levels, rows, LANES), f32),
            pltpu.SemaphoreType.DMA((1 + 2 * PIECES,)),
        ],
        compiler_params=params,
        cost_estimate=pl.CostEstimate(flops=2 * 10**9, bytes_accessed=10**6, transcendentals=10**5),
        name="own_tile",
    )(u_wind, theta, klass, diff_table, sent)
    packed = pl.pallas_call(
        functools.partial(pack_kernel, slabs),
        out_shape=jax.ShapeDtypeStruct((slabs, 120, LANES), f32),
        compiler_params=params,
        name="pack",
    )(sums, straight, diagonal)
    got = lax.all_to_all(packed, "gz", 0, 0)
    return pl.pallas_call(
        functools.partial(last_kernel, slabs),
        out_shape=[jax.ShapeDtypeStruct(u_wind.shape, f32)] * 2,
        in_specs=[vmem] * 7,
        out_specs=[hbm] * 2,
        scratch_shapes=[
            pltpu.VMEM(acc_shape, f32),
            pltpu.VMEM(((SPARE + 1) * 32, LANES), f32),
            pltpu.VMEM((levels + 2 * CLASSES, FINE, LANES), f32),
            pltpu.VMEM((3 * LANES, LANES), f32),
            pltpu.VMEM((2, levels, rows, LANES), f32),
            field,
            field,
            pltpu.SMEM((SPARE + 1,), jnp.int32),
            pltpu.SMEM((2 * SPARE + 2,), jnp.int32),
            pltpu.SMEM((8 * SPARE,), jnp.int32),
            pltpu.SemaphoreType.DMA((2, PIECES)),
        ],
        compiler_params=params,
        name="solve",
    )(got, own, u_here, theta_here, index, picks, mix)


def solution(mesh):
    return jax.shard_map(
        shards,
        mesh=mesh,
        in_specs=(
            P("gz", "gx", "gy"),
            P("gz", "gx", "gy"),
            P(None, "gx", "gy", None),
            P("gx", "gy"),
            P("gx", "gy"),
            P(),
        ),
        out_specs=(P("gz", "gx", "gy"), P("gz", "gx", "gy")),
        check_vma=False,
    )
```
